128 devices in a mesh: rows: 128 (over z, x, y, core).
Axes of the slice: x: 4, y: 4, z: 4, core: 2. Of those that a mesh axis runs over, the one named last changes fastest.
Arguments:
- matrix: float32 [2097152, 128], P('rows'), may hold values from -60 to 60, as said below
- signs: int32 [2097152], P('rows'), may hold values from -1 to 1, as said below
- sample_rows: int32 [32768], P('rows'), may hold values from 0 to 2097151, as said below
Outputs:
- sketch: float32 [32768, 128], P('rows')
- r_factors: float32 [16, 128, 128], replicated
The draws below stay inside these ranges and needn't reach their ends.
Inputs may be any that keep to these rules, and one draw needn't show every extreme that they name: `matrix`: every entry is finite. `signs`: every entry is -1 or 1. `sample_rows`: entries are ascending within each device's 2 entries from one source range, and each block of 256 entries (one device's share) takes exactly 2 entries from each device's range of 16384 matrix rows, in device order; within such a block, exactly 2 entries have an offset inside their range (index modulo 16384) in each of the 128 aligned offset intervals of length 128; repeats may occur.
All inputs are finite; a program needn't handle non-finite values.
Results may differ from the reference program's by a relative error of at most 0.00013.
Values sent between devices are 32-bit elements; how exact they have to be, the bound alone decides.
A program may use at most 128 MiB of HBM per device.

```python
import math
import jax
import jax.numpy as jnp
from jax import lax

C = 128
R_DEV = 16384
SAMP_OWN = 2048
SAMP_DEV = 256
SAMP_PAIR = 2
OWNERS = 16
ROWS = 2097152
SAMPLES = 32768


def draw_matrix(key, part):
    key = jax.random.fold_in(key, 11)
    key_base, key_cols, key_rows = jax.random.split(key, 3)
    base = jnp.clip(jax.random.normal(key_base, (ROWS, C), jnp.float32), -6.0, 6.0)
    col_scale = jnp.exp(jax.random.uniform(key_cols, (C,), jnp.float32, math.log(0.5), math.log(5.0)))
    row_scale = jnp.exp(jax.random.uniform(key_rows, (ROWS, 1), jnp.float32, math.log(0.5), math.log(2.0)))
    return base * row_scale * col_scale[None, :]


def draw_signs(key, part):
    key = jax.random.fold_in(key, 22)
    return 2 * jax.random.randint(key, (ROWS,), 0, 2, jnp.int32) - 1


def draw_sample_rows(key, part):
    key = jax.random.fold_in(key, 33)
    key_shift, key_inner = jax.random.split(key)
    targets = SAMPLES // SAMP_DEV
    sources = SAMP_DEV // SAMP_PAIR
    width_piece = R_DEV // sources
    shifts = jax.random.randint(key_shift, (targets,), 0, sources, jnp.int32)
    shifts = shifts.at[0].set(0).at[targets - 1].set(0)
    serial = jnp.arange(sources, dtype=jnp.int32)[:, None] * SAMP_PAIR + jnp.arange(SAMP_PAIR, dtype=jnp.int32)[None, :]
    pieces = (serial[None, :, :] + shifts[:, None, None]) % sources
    inner = jax.random.randint(key_inner, (targets, sources, SAMP_PAIR), 0, width_piece, jnp.int32)
    inner = inner.at[0, 0, 0].set(0)
    inner = inner.at[targets - 1, sources - 1, SAMP_PAIR - 1].set(width_piece - 1)
    offsets = jnp.sort(pieces * width_piece + inner, axis=-1)
    starts = (jnp.arange(sources, dtype=jnp.int32) * R_DEV)[None, :, None]
    return (offsets + starts).reshape(-1)


def setup_inputs(seed: int = 0) -> dict:
    key_list = jax.random.split(jax.random.key(seed), 4)
    matrix = draw_matrix(jax.random.fold_in(key_list[3], 71), 0)
    signs = draw_signs(jax.random.fold_in(key_list[3], 71), 0)
    sample_rows = draw_sample_rows(jax.random.fold_in(key_list[3], 71), 0)
    return dict(matrix=matrix, signs=signs, sample_rows=sample_rows)


def reference(matrix, signs, sample_rows):
    field = matrix * signs.astype(jnp.float32)[:, None] * (1.0 / math.sqrt(ROWS))
    for section in range(ROWS.bit_length() - 1):
        span = 2 ** section
        shaped = field.reshape(ROWS // (2 * span), 2, span, C)
        field = jnp.stack([shaped[:, 0] + shaped[:, 1], shaped[:, 0] - shaped[:, 1]], axis=1).reshape(ROWS, C)
    sketch = jnp.take(field, sample_rows, axis=0)
    blocks = sketch.reshape(OWNERS, SAMP_OWN, C)
    grams = jnp.einsum('osc,osd->ocd', blocks, blocks, precision=lax.Precision.HIGHEST)
    lower = jnp.linalg.cholesky(grams / SAMP_OWN)
    return (sketch, jnp.swapaxes(lower, 1, 2))
```

```python
import functools
import math

import jax
import jax.numpy as jnp
from jax import lax
from jax.experimental import pallas as pl
from jax.experimental.pallas import tpu as pltpu
from jax.sharding import PartitionSpec as P

MESH = pl.DeviceIdType.MESH
F32 = jnp.float32
BF16 = jnp.bfloat16
I32 = jnp.int32

TICKS = 8
STREAMS = 4
ROWS = 2097152
SAMP_OWN = 2048


def dot_tt(lhs, rhs, precision=None):
    return lax.dot_general(
        lhs, rhs, (((0,), (0,)), ((), ())), precision=precision, preferred_element_type=F32
    )


def iota(shape, dim):
    return lax.broadcasted_iota(I32, shape, dim)


def odd(bits):
    bits = bits ^ (bits >> 4)
    bits = bits ^ (bits >> 2)
    bits = bits ^ (bits >> 1)
    return bits & 1


def split2(value):
    high = value.astype(BF16)
    return high, (value - high.astype(F32)).astype(BF16)


def split3(value):
    high = value.astype(BF16)
    rest = value - high.astype(F32)
    mid = rest.astype(BF16)
    return high, mid, (rest - mid.astype(F32)).astype(BF16)


def kernel(
    matrix_ref, signs_ref, samples_ref, sketch_ref, factors_ref,
    X, SIB, P1, R1, R2, R3, R4, T3, R5, Y8, IDX, ML, SO, SS, POS, WF, WALL, G, RG1, RG2, GF, U, OUT,
    load_sem, y_send, y_recv, x_send, x_recv, z_send, z_recv, sib_send, sib_recv,
    s1, r1, s2, r2, s3, r3, s4, r4, s5, r5,
    w_send, w_recv, g1_send, g1_recv, g2_send, g2_recv, g3_send, g3_recv,
    ax_send, ax_recv, az_send, az_recv, ay_send, ay_recv, ac_send, ac_recv, out_sem,
):
    me = lax.axis_index("rows")
    core = me % 2
    y_pos = (me // 2) % 4
    x_pos = (me // 8) % 4
    z_pos = me // 32
    sibling = me + 1 - 2 * core

    def along(stride, hop):
        pos = (me // stride) % 4
        return me + ((pos + hop) % 4 - pos) * stride

    def axis_of(order, stage):
        k = (order + stage) % 3
        stride = 32 - 33 * k + 9 * k * k
        return stride, (me // stride) % 4

    def send(src, dst, send_sem, recv_sem, device):
        copy = pltpu.make_async_remote_copy(
            src_ref=src, dst_ref=dst, send_sem=send_sem, recv_sem=recv_sem,
            device_id=(device,), device_id_type=MESH,
        )
        copy.start()

    def wait(ref, sem):
        pltpu.make_async_copy(ref, ref, sem).wait()

    def load(chunk):
        return pltpu.make_async_copy(matrix_ref.at[chunk], X.at[chunk], load_sem.at[chunk])

    for chunk in range(16):
        load(chunk).start()

    group = [(dy, dc) for dy in range(4) for dc in range(2) if (dy, dc) != (0, 0)]

    def mate(dy, dc):
        return along(2, dy) + dc * (1 - 2 * core)

    barrier = pltpu.get_barrier_semaphore()
    for dy, dc in group:
        pl.semaphore_signal(barrier, inc=1, device_id=(mate(dy, dc),), device_id_type=MESH)
    for hop in (1, 2, 3):
        pl.semaphore_signal(barrier, inc=1, device_id=(along(8, hop),), device_id_type=MESH)
        pl.semaphore_signal(barrier, inc=1, device_id=(along(32, hop),), device_id_type=MESH)

    samples = samples_ref[...]
    part = (samples >> 7) & 127
    intervals = jnp.concatenate([part[0:1], part[1:2]], axis=1)
    values = jnp.concatenate([samples[0:1], samples[1:2]], axis=1)
    onehot = iota((128, 256), 0) == intervals
    onehot_f = jnp.where(onehot, 1.0, 0.0)
    before = jnp.where(iota((256, 256), 0) < iota((256, 256), 1), 1.0, 0.0).astype(BF16)
    count = jnp.dot(onehot_f.astype(BF16), before, preferred_element_type=F32)
    rank = jnp.sum(count * onehot_f, axis=0, keepdims=True).astype(I32)
    place = (
        (intervals >> 6) * 128 + (intervals & 7) * 16 + ((intervals >> 3) & 7) * 2 + rank
    )
    POS[...] = place
    slot = rank * 128 + intervals
    chosen = jnp.where(iota((256, 256), 0) == slot, 1.0, 0.0).astype(BF16)
    row8 = iota((8, 256), 0)
    fields = jnp.where(row8 == 0, values & 127, jnp.where(row8 == 1, values >> 14, 0))
    sorted_fields = lax.dot_general(
        fields.astype(F32).astype(BF16), chosen, (((1,), (1,)), ((), ())), preferred_element_type=F32
    ).astype(I32)
    sorted_rows = (
        sorted_fields[1:2] * 16384 + (iota((1, 256), 1) & 127) * 128 + sorted_fields[0:1]
    )
    mine8 = 2 * y_pos + core
    Y8[mine8, 0:1, :] = sorted_rows[:, :128]
    Y8[mine8, 1:2, :] = sorted_rows[:, 128:]
    pl.semaphore_wait(barrier, 13)
    for n, (dy, dc) in enumerate(group):
        send(Y8.at[mine8], Y8.at[mine8], y_send.at[n], y_recv.at[n], mate(dy, dc))

    had = (1 - 2 * odd(iota((128, 128), 0) & iota((128, 128), 1))).astype(F32)

    def front(chunk, carry):
        load(chunk).wait()
        for al in range(8):
            high, low = split2(X[chunk, al])
            sign = signs_ref[pl.ds(chunk * 8 + al, 1), :].astype(F32)
            signed = (had * sign).astype(BF16)
            X[chunk, al] = jnp.dot(
                jnp.concatenate([signed, signed], axis=1),
                jnp.concatenate([high, low], axis=0),
                preferred_element_type=F32,
            )
        for tile in range(16):
            rows = slice(8 * tile, 8 * tile + 8)
            v = [X[chunk, al, rows, :] for al in range(8)]
            for span in (1, 2, 4):
                v = butterfly(v, span)
            for al in range(8):
                X[chunk, al, rows, :] = v[al]
        return carry

    def butterfly(v, span):
        out = list(v)
        for n in range(len(v)):
            if n & span == 0:
                out[n] = v[n] + v[n + span]
                out[n + span] = v[n] - v[n + span]
        return out

    lax.fori_loop(0, 5, front, 0)
    for n in range(7):
        wait(Y8.at[0], y_recv.at[n])
    for q in range(8):
        for j in range(2):
            IDX[z_pos, x_pos, j, q : q + 1, :] = Y8[q, j : j + 1, :]
    for hop in (1, 2, 3):
        block = IDX.at[z_pos, x_pos]
        send(block, block, x_send.at[hop - 1], x_recv.at[hop - 1], along(8, hop))
    lax.fori_loop(5, 10, front, 0)
    for hop in (1, 2, 3):
        wait(IDX.at[0, 0], x_recv.at[hop - 1])
    for hop in (1, 2, 3):
        block = IDX.at[z_pos]
        send(block, block, z_send.at[hop - 1], z_recv.at[hop - 1], along(32, hop))
    lax.fori_loop(10, 16, front, 0)

    def second(step):
        def tile_step(tile, carry):
            rows = pl.ds(pl.multiple_of(tile * 8, 8), 8)
            v = [X[ah, step, rows, :] for ah in range(16)]
            for span in (1, 2, 4, 8):
                v = butterfly(v, span)
            for ah in range(16):
                X[ah, step, rows, :] = v[ah]
            return carry

        lax.fori_loop(0, 16, tile_step, 0)
        send(
            X.at[pl.ds((1 - core) * 8, 8), step], SIB.at[step], sib_send.at[step], sib_recv.at[step], sibling
        )

    second(0)

    for hop in (1, 2, 3):
        wait(IDX.at[0], z_recv.at[hop - 1])
    from_t = iota((128, 128), 0)
    to_t = iota((128, 128), 1)
    hi_t, mid_t, lo_t, core_t = to_t // 32, (to_t // 8) % 4, (to_t // 2) % 4, to_t % 2
    natural = [
        hi_t * 32 + mid_t * 8 + lo_t * 2 + core_t,
        hi_t * 8 + mid_t * 2 + lo_t * 32 + core_t,
        hi_t * 2 + mid_t * 32 + lo_t * 8 + core_t,
    ]
    for order in range(3):
        perm = jnp.where(from_t == natural[order], 1.0, 0.0).astype(BF16)
        for j in range(2):
            rows = IDX[:, :, j].reshape(128, 128)
            low = (rows & 127).astype(F32).astype(BF16)
            block = (rows >> 14).astype(F32).astype(BF16)
            ML[order, j] = dot_tt(low, perm).astype(I32)
            owner = dot_tt(block, perm).astype(I32)
            SO[order, j] = (1 - 2 * odd(owner & me)).astype(F32)
            SS[order, j] = (1 - 2 * odd(owner & sibling)).astype(F32)

    sub = iota((128, 128), 0)

    def order_of(s, tick):
        return s if s < 3 else tick % 3

    def produce(tick):
        def one(n, carry):
            s = n // 2
            order = s + (s // 3) * (tick % 3 - 3)
            p = (core * 8 + n) * 8 + tick
            own_hi, own_lo = split2(X[core * 8 + n, tick])
            sib_hi, sib_lo = split2(SIB[tick, n])
            picks = []
            for j in range(2):
                hit = sub == ML[order, j, pl.ds(p, 1), :]
                own = jnp.where(hit, SO[order, j, pl.ds(p, 1), :], 0.0).astype(BF16)
                sib = jnp.where(hit, SS[order, j, pl.ds(p, 1), :], 0.0).astype(BF16)
                picks.append(jnp.concatenate([own, sib], axis=0))
            pick = jnp.concatenate(picks, axis=1)
            got = dot_tt(pick, jnp.concatenate([own_hi, sib_hi], axis=0))
            got = got + dot_tt(pick, jnp.concatenate([own_lo, sib_lo], axis=0))
            P1[tick, s, n % 2] = got.reshape(2, 4, 4, 8, 128)
            return carry

        lax.fori_loop(0, 8, one, 0)

    def first_send(tick):
        for s in range(STREAMS):
            stride, a = axis_of(order_of(s, tick), 0)
            far = (a + 2) % 4
            send(P1.at[tick, s, :, 0, far], R1.at[tick, s, 0], s1.at[tick], r1.at[tick], along(stride, 1))
            send(P1.at[tick, s, :, 1, far], R1.at[tick, s, 1], s1.at[tick], r1.at[tick], along(stride, 3))

    def first_pass(tick):
        wait(R1.at[tick], r1.at[tick])
        for s in range(STREAMS):
            stride, a = axis_of(order_of(s, tick), 0)
            up, down = (a + 1) % 4, (a + 3) % 4
            P1[tick, s, :, 0, up] += R1[tick, s, 0]
            P1[tick, s, :, 1, down] += R1[tick, s, 1]
            send(P1.at[tick, s, :, :, up], R2.at[tick, s, 0], s2.at[tick], r2.at[tick], along(stride, 1))
            send(P1.at[tick, s, :, :, down], R2.at[tick, s, 1], s2.at[tick], r2.at[tick], along(stride, 3))

    def second_send(tick):
        wait(R2.at[tick], r2.at[tick])
        for s in range(STREAMS):
            _, a = axis_of(order_of(s, tick), 0)
            P1[tick, s, :, :, a] += R2[tick, s, 0] + R2[tick, s, 1]
            stride, b = axis_of(order_of(s, tick), 1)
            far = (b + 2) % 4
            send(P1.at[tick, s, :, 0, a, far], R3.at[tick, s, 0], s3.at[tick], r3.at[tick], along(stride, 1))
            send(P1.at[tick, s, :, 1, a, far], R3.at[tick, s, 1], s3.at[tick], r3.at[tick], along(stride, 3))

    def second_pass(tick):
        wait(R3.at[tick], r3.at[tick])
        for s in range(STREAMS):
            _, a = axis_of(order_of(s, tick), 0)
            stride, b = axis_of(order_of(s, tick), 1)
            up, down = (b + 1) % 4, (b + 3) % 4
            P1[tick, s, :, 0, a, up] += R3[tick, s, 0]
            P1[tick, s, :, 1, a, down] += R3[tick, s, 1]
            send(P1.at[tick, s, :, :, a, up], R4.at[tick, s, 0], s4.at[tick], r4.at[tick], along(stride, 1))
            send(P1.at[tick, s, :, :, a, down], R4.at[tick, s, 1], s4.at[tick], r4.at[tick], along(stride, 3))

    def third_send(tick):
        wait(R4.at[tick], r4.at[tick])
        for s in range(STREAMS):
            _, a = axis_of(order_of(s, tick), 0)
            _, b = axis_of(order_of(s, tick), 1)
            total = P1[tick, s, :, :, a, b] + R4[tick, s, 0] + R4[tick, s, 1]
            for g in range(2):
                for j in range(2):
                    for q in range(4):
                        for ct in range(2):
                            row = ct * 4 + g * 2 + j
                            T3[tick, s, q, row : row + 1, :] = total[g, j, 2 * q + ct : 2 * q + ct + 1, :]
            stride, d = axis_of(order_of(s, tick), 2)
            for hop in (1, 2, 3):
                send(
                    T3.at[tick, s, (d + hop) % 4], R5.at[tick, s, hop - 1], s5.at[tick], r5.at[tick],
                    along(stride, hop),
                )

    scale = 1.0 / math.sqrt(ROWS)

    def last(tick):
        wait(R5.at[tick], r5.at[tick])
        done = []
        for s in range(STREAMS):
            _, d = axis_of(order_of(s, tick), 2)
            done.append((T3[tick, s, d] + R5[tick, s, 0] + R5[tick, s, 1] + R5[tick, s, 2]) * scale)
        for ct in range(2):
            for pair in range(2):
                rows = pl.ds(pl.multiple_of(tick * 16 + pair * 8, 8), 8)
                WF[ct, rows, :] = jnp.concatenate(
                    [done[2 * pair][4 * ct : 4 * ct + 4], done[2 * pair + 1][4 * ct : 4 * ct + 4]], axis=0
                )

    def tick_step(i, carry):
        @pl.when(i + 1 < TICKS)
        def _():
            second(i + 1)

        @pl.when(i < TICKS)
        def _():
            wait(SIB.at[i], sib_recv.at[i])
            produce(i)
            first_send(i)

        for lag, work in enumerate((first_pass, second_send, second_pass, third_send, last), 1):

            @pl.when((i >= lag) & (i < TICKS + lag))
            def _():
                work(i - lag)

        return carry

    lax.fori_loop(0, TICKS + 5, tick_step, 0)

    send(WF.at[1 - core], WALL.at[core], w_send, w_recv, sibling)
    mine = WF[...].reshape(256, 128)
    gram = dot_tt(mine, mine, lax.Precision.HIGHEST) * (1.0 / SAMP_OWN)
    G[...] = gram.reshape(2, 4, 16, 128)
    send(G.at[1 - core], RG1, g1_send, g1_recv, sibling)
    wait(RG1, g1_recv)
    wait(G.at[0], g1_send)
    G[core] += RG1[...]
    for hop in (1, 2, 3):
        send(G.at[core, (y_pos + hop) % 4], RG2.at[hop - 1], g2_send.at[hop - 1], g2_recv.at[hop - 1], along(2, hop))
    for hop in (1, 2, 3):
        wait(RG2.at[0], g2_recv.at[hop - 1])
    GF[core, y_pos] = G[core, y_pos] + RG2[0] + RG2[1] + RG2[2]
    block = GF.at[core, y_pos]
    for n, (dy, dc) in enumerate(group):
        send(block, block, g3_send.at[n], g3_recv.at[n], mate(dy, dc))
    for n in range(7):
        wait(GF.at[0, 0], g3_recv.at[n])

    sub8 = iota((8, 128), 0)
    lane8 = iota((8, 128), 1)
    work = GF[...].reshape(128, 128)
    for kb in range(16):
        panel = work[:8]
        for j in range(8):
            col = panel[:, 8 * kb + j : 8 * kb + j + 1]
            inv = lax.rsqrt(col[j : j + 1])
            row = panel[j : j + 1] * inv
            panel = jnp.where(sub8 > j, panel - (col * inv) * row, jnp.where(sub8 == j, row, panel))
        panel = jnp.where(lane8 >= 8 * kb + sub8, panel, 0.0)
        U[8 * kb : 8 * kb + 8, :] = panel
        if kb < 15:
            update = dot_tt(panel, panel, lax.Precision.HIGHEST)
            work = work[8:] - update[8 * kb + 8 :]

    OUT[z_pos, x_pos, core, y_pos] = U[pl.ds(pl.multiple_of(core * 64 + y_pos * 16, 16), 16), :]
    block = OUT.at[z_pos, x_pos, core, y_pos]
    for hop in (1, 2, 3):
        send(block, block, ax_send.at[hop - 1], ax_recv.at[hop - 1], along(8, hop))

    WALL[core] = WF[core]
    wait(WALL.at[0], w_recv)
    back = jnp.where(iota((256, 256), 0) == POS[...], 1.0, 0.0).astype(BF16)
    sketch_ref[...] = sum(dot_tt(back, term) for term in split3(WALL[...].reshape(256, 128)))

    for hop in (1, 2, 3):
        wait(OUT.at[0, 0, 0, 0], ax_recv.at[hop - 1])
    block = OUT.at[z_pos, :, core, y_pos]
    for hop in (1, 2, 3):
        send(block, block, az_send.at[hop - 1], az_recv.at[hop - 1], along(32, hop))
    for hop in (1, 2, 3):
        wait(OUT.at[0, :, 0, 0], az_recv.at[hop - 1])
    block = OUT.at[:, :, core, y_pos]
    for hop in (1, 2, 3):
        send(block, block, ay_send.at[hop - 1], ay_recv.at[hop - 1], along(2, hop))
    for hop in (1, 2, 3):
        wait(OUT.at[:, :, 0, 0], ay_recv.at[hop - 1])
    block = OUT.at[:, :, core]
    send(block, block, ac_send, ac_recv, sibling)
    wait(OUT.at[:, :, 0], ac_recv)
    final = pltpu.make_async_copy(OUT, factors_ref, out_sem)
    final.start()

    for n in range(7):
        wait(Y8.at[0], y_send.at[n])
        wait(GF.at[0, 0], g3_send.at[n])
    for n in range(3):
        wait(IDX.at[0, 0], x_send.at[n])
        wait(IDX.at[0], z_send.at[n])
        wait(RG2.at[0], g2_send.at[n])
        wait(OUT.at[0, 0, 0, 0], ax_send.at[n])
        wait(OUT.at[0, :, 0, 0], az_send.at[n])
        wait(OUT.at[:, :, 0, 0], ay_send.at[n])
    wait(OUT.at[:, :, 0], ac_send)
    wait(WALL.at[0], w_send)

    def sent(tick, carry):
        wait(SIB.at[tick], sib_send.at[tick])
        wait(R1.at[tick], s1.at[tick])
        wait(R2.at[tick], s2.at[tick])
        wait(R3.at[tick], s3.at[tick])
        wait(R4.at[tick], s4.at[tick])
        wait(R5.at[tick], s5.at[tick])
        return carry

    lax.fori_loop(0, TICKS, sent, 0)
    final.wait()


def body(matrix, signs, samples):
    dma = pltpu.SemaphoreType.DMA
    vmem = pltpu.VMEM
    t, s = TICKS, STREAMS
    sketch, factors = pl.pallas_call(
        kernel,
        out_shape=(
            jax.ShapeDtypeStruct((256, 128), F32),
            jax.ShapeDtypeStruct((4, 4, 2, 4, 16, 128), F32),
        ),
        in_specs=[
            pl.BlockSpec(memory_space=pl.ANY),
            pl.BlockSpec(memory_space=pltpu.VMEM),
            pl.BlockSpec(memory_space=pltpu.VMEM),
        ],
        out_specs=(pl.BlockSpec(memory_space=pltpu.VMEM), pl.BlockSpec(memory_space=pl.ANY)),
        scratch_shapes=[
            vmem((16, 8, 128, 128), F32),
            vmem((8, 8, 128, 128), F32),
            vmem((t, s, 2, 2, 4, 4, 8, 128), F32),
            vmem((t, s, 2, 2, 4, 8, 128), F32),
            vmem((t, s, 2, 2, 2, 4, 8, 128), F32),
            vmem((t, s, 2, 2, 8, 128), F32),
            vmem((t, s, 2, 2, 2, 8, 128), F32),
            vmem((t, s, 4, 8, 128), F32),
            vmem((t, s, 3, 8, 128), F32),
            vmem((8, 8, 128), I32),
            vmem((4, 4, 2, 8, 128), I32),
            vmem((3, 2, 128, 128), I32),
            vmem((3, 2, 128, 128), F32),
            vmem((3, 2, 128, 128), F32),
            vmem((1, 256), I32),
            vmem((2, 128, 128), F32),
            vmem((2, 128, 128), F32),
            vmem((2, 4, 16, 128), F32),
            vmem((4, 16, 128), F32),
            vmem((3, 16, 128), F32),
            vmem((2, 4, 16, 128), F32),
            vmem((128, 128), F32),
            vmem((4, 4, 2, 4, 16, 128), F32),
            dma((16,)), dma((7,)), dma((7,)), dma((3,)), dma((3,)), dma((3,)), dma((3,)),
            dma((t,)), dma((t,)),
            dma((t,)), dma((t,)), dma((t,)), dma((t,)), dma((t,)), dma((t,)), dma((t,)), dma((t,)),
            dma((t,)), dma((t,)),
            dma(()), dma(()), dma(()), dma(()), dma((3,)), dma((3,)), dma((7,)), dma((7,)),
            dma((3,)), dma((3,)), dma((3,)), dma((3,)), dma((3,)), dma((3,)), dma(()), dma(()), dma(()),
        ],
        compiler_params=pltpu.CompilerParams(
            collective_id=0, has_side_effects=True, vmem_limit_bytes=48 * 1024 * 1024
        ),
    )(matrix.reshape(16, 8, 128, 128), signs.reshape(128, 128), samples.reshape(2, 128))
    return sketch, factors.reshape(16, 128, 128)


def solution(mesh):
    return jax.shard_map(
        body,
        mesh=mesh,
        in_specs=(P("rows", None), P("rows"), P("rows")),
        out_specs=(P("rows", None), P()),
        check_vma=False,
    )
```

```python
import functools
import math

import jax
import jax.numpy as jnp
from jax import lax
from jax.experimental import pallas as pl
from jax.experimental.pallas import tpu as pltpu
from jax.sharding import PartitionSpec as P

MESH = pl.DeviceIdType.MESH
F32 = jnp.float32
BF16 = jnp.bfloat16
I32 = jnp.int32

TICKS = 8
LAG = 2
DIRECT = 2
STREAMS = 4
ROWS = 2097152
SAMP_OWN = 2048


def dot_tt(lhs, rhs, precision=None):
    return lax.dot_general(
        lhs, rhs, (((0,), (0,)), ((), ())), precision=precision, preferred_element_type=F32
    )


def iota(shape, dim):
    return lax.broadcasted_iota(I32, shape, dim)


def odd(bits):
    bits = bits ^ (bits >> 4)
    bits = bits ^ (bits >> 2)
    bits = bits ^ (bits >> 1)
    return bits & 1


def split2(value):
    high = value.astype(BF16)
    return high, (value - high.astype(F32)).astype(BF16)


def split3(value):
    high = value.astype(BF16)
    rest = value - high.astype(F32)
    mid = rest.astype(BF16)
    return high, mid, (rest - mid.astype(F32)).astype(BF16)


def kernel(
    matrix_ref, signs_ref, samples_ref, sketch_ref, factors_ref,
    X, SIB, P1, R1, R2, R3, R4, T3, R5, Y8, IDX, SGN, SMP, ML, SO, SS, POS, WF, WALL, G, RG1, RG2, GF, OUT, DUM,
    load_sem, in_sem, y_send, y_recv, p_send, p_recv, sib_send, sib_recv,
    s1, r1, s2, r2, s3, r3, s4, r4, s5, r5,
    w_send, w_recv, g1_send, g1_recv, g2_send, g2_recv, g3_send, g3_recv,
    o_send, o_recv, f_send, f_recv, out_sem,
):
    me = lax.axis_index("rows")
    core = me % 2
    y_pos = (me // 2) % 4
    x_pos = (me // 8) % 4
    z_pos = me // 32
    sibling = me + 1 - 2 * core

    def along(stride, hop):
        pos = (me // stride) % 4
        return me + ((pos + hop) % 4 - pos) * stride

    def axis_of(order, stage):
        k = (order + stage) % 3
        stride = 32 - 33 * k + 9 * k * k
        return stride, (me // stride) % 4

    def send(src, dst, send_sem, recv_sem, device):
        copy = pltpu.make_async_remote_copy(
            src_ref=src, dst_ref=dst, send_sem=send_sem, recv_sem=recv_sem,
            device_id=(device,), device_id_type=MESH,
        )
        copy.start()

    def wait(ref, sem):
        pltpu.make_async_copy(ref, ref, sem).wait()

    def load(chunk):
        return pltpu.make_async_copy(matrix_ref.at[chunk], X.at[chunk], load_sem.at[chunk])

    fetch_samples = pltpu.make_async_copy(samples_ref, SMP, in_sem.at[0])
    fetch_samples.start()
    fetch_signs = pltpu.make_async_copy(signs_ref, SGN, in_sem.at[1])
    fetch_signs.start()
    for chunk in range(16):
        load(chunk).start()

    group = [(dy, dc) for dy in range(4) for dc in range(2) if (dy, dc) != (0, 0)]
    plane = [(dz, dx) for dz in range(4) for dx in range(4) if (dz, dx) != (0, 0)]

    def mate(dy, dc):
        return along(2, dy) + dc * (1 - 2 * core)

    def peer(dz, dx):
        return ((z_pos + dz) % 4) * 32 + ((x_pos + dx) % 4) * 8 + me % 8

    barrier = pltpu.get_barrier_semaphore()
    for dy, dc in group:
        pl.semaphore_signal(barrier, inc=1, device_id=(mate(dy, dc),), device_id_type=MESH)
    for dz, dx in plane:
        pl.semaphore_signal(barrier, inc=1, device_id=(peer(dz, dx),), device_id_type=MESH)

    had = (1 - 2 * odd(iota((128, 128), 0) & iota((128, 128), 1))).astype(F32)
    fetch_samples.wait()

    samples = SMP[...]
    part = (samples >> 7) & 127
    intervals = jnp.concatenate([part[0:1], part[1:2]], axis=1)
    values = jnp.concatenate([samples[0:1], samples[1:2]], axis=1)
    onehot = iota((128, 256), 0) == intervals
    onehot_f = jnp.where(onehot, 1.0, 0.0)
    before = jnp.where(iota((256, 256), 0) < iota((256, 256), 1), 1.0, 0.0).astype(BF16)
    count = jnp.dot(onehot_f.astype(BF16), before, preferred_element_type=F32)
    rank = jnp.sum(count * onehot_f, axis=0, keepdims=True).astype(I32)
    place = (
        (intervals >> 6) * 128 + (intervals & 7) * 16 + ((intervals >> 3) & 7) * 2 + rank
    )
    POS[...] = place
    slot = rank * 128 + intervals
    chosen = jnp.where(iota((256, 256), 0) == slot, 1.0, 0.0).astype(BF16)
    row8 = iota((8, 256), 0)
    fields = jnp.where(row8 == 0, values & 127, jnp.where(row8 == 1, values >> 14, 0))
    sorted_fields = lax.dot_general(
        fields.astype(F32).astype(BF16), chosen, (((1,), (1,)), ((), ())), preferred_element_type=F32
    ).astype(I32)
    sorted_rows = (
        sorted_fields[1:2] * 16384 + (iota((1, 256), 1) & 127) * 128 + sorted_fields[0:1]
    )
    mine8 = 2 * y_pos + core
    Y8[mine8, 0:1, :] = sorted_rows[:, :128]
    Y8[mine8, 1:2, :] = sorted_rows[:, 128:]
    def front(chunk, carry):
        load(chunk).wait()
        for al in range(8):
            high, low = split2(X[chunk, al])
            sign = SGN[pl.ds(chunk * 8 + al, 1), :].astype(F32)
            signed = (had * sign).astype(BF16)
            X[chunk, al] = jnp.dot(
                jnp.concatenate([signed, signed], axis=1),
                jnp.concatenate([high, low], axis=0),
                preferred_element_type=F32,
            )
        for tile in range(16):
            rows = slice(8 * tile, 8 * tile + 8)
            v = [X[chunk, al, rows, :] for al in range(8)]
            for span in (1, 2, 4):
                v = butterfly(v, span)
            for al in range(8):
                X[chunk, al, rows, :] = v[al]
        return carry

    def butterfly(v, span):
        out = list(v)
        for n in range(len(v)):
            if n & span == 0:
                out[n] = v[n] + v[n + span]
                out[n + span] = v[n] - v[n + span]
        return out

    fetch_signs.wait()
    lax.fori_loop(0, 3, front, 0)
    pl.semaphore_wait(barrier, 22)
    for n, (dy, dc) in enumerate(group):
        send(Y8.at[mine8], Y8.at[mine8], y_send.at[n], y_recv.at[n], mate(dy, dc))
    lax.fori_loop(3, 10, front, 0)
    for n in range(7):
        wait(Y8.at[0], y_recv.at[n])
    for q in range(8):
        for j in range(2):
            IDX[z_pos, x_pos, j, q : q + 1, :] = Y8[q, j : j + 1, :]
    for dz, dx in plane:
        send(IDX.at[z_pos, x_pos], IDX.at[z_pos, x_pos], p_send, p_recv, peer(dz, dx))
    lax.fori_loop(10, 16, front, 0)

    def second(step):
        def tile_step(tile, carry):
            rows = pl.ds(pl.multiple_of(tile * 8, 8), 8)
            v = [X[ah, step, rows, :] for ah in range(16)]
            for span in (1, 2, 4, 8):
                v = butterfly(v, span)
            for ah in range(16):
                X[ah, step, rows, :] = v[ah]
            return carry

        lax.fori_loop(0, 16, tile_step, 0)
        send(
            X.at[pl.ds((1 - core) * 8, 8), step], SIB.at[step], sib_send.at[step], sib_recv.at[step], sibling
        )

    for step in range(TICKS):
        second(step)

    wait(DUM, p_recv)
    from_t = iota((128, 128), 0)
    to_t = iota((128, 128), 1)
    hi_t, mid_t, lo_t, core_t = to_t // 32, (to_t // 8) % 4, (to_t // 2) % 4, to_t % 2
    natural = [
        hi_t * 32 + mid_t * 8 + lo_t * 2 + core_t,
        hi_t * 8 + mid_t * 2 + lo_t * 32 + core_t,
        hi_t * 2 + mid_t * 32 + lo_t * 8 + core_t,
    ]
    for order in range(3):
        perm = jnp.where(from_t == natural[order], 1.0, 0.0).astype(BF16)
        for j in range(2):
            rows = IDX[:, :, j].reshape(128, 128)
            low = (rows & 127).astype(F32).astype(BF16)
            block = (rows >> 14).astype(F32).astype(BF16)
            ML[order, j] = dot_tt(low, perm).astype(I32)
            owner = dot_tt(block, perm).astype(I32)
            SO[order, j] = (1 - 2 * odd(owner & me)).astype(F32)
            SS[order, j] = (1 - 2 * odd(owner & sibling)).astype(F32)

    sub = iota((128, 128), 0)

    def order_of(s, tick):
        return s if s < 3 else tick % 3

    def produce(tick):
        def one(n, carry):
            s = n // 2
            order = s + (s // 3) * (tick % 3 - 3)
            p = (core * 8 + n) * 8 + tick
            own_hi, own_lo = split2(X[core * 8 + n, tick])
            sib_hi, sib_lo = split2(SIB[tick, n])
            picks = []
            for j in range(2):
                hit = sub == ML[order, j, pl.ds(p, 1), :]
                own = jnp.where(hit, SO[order, j, pl.ds(p, 1), :], 0.0).astype(BF16)
                sib = jnp.where(hit, SS[order, j, pl.ds(p, 1), :], 0.0).astype(BF16)
                picks.append(jnp.concatenate([own, sib], axis=0))
            pick = jnp.concatenate(picks, axis=1)
            terms = jnp.concatenate(
                [jnp.concatenate([own_hi, sib_hi], axis=0), jnp.concatenate([own_lo, sib_lo], axis=0)], axis=1
            )
            got = dot_tt(pick, terms)
            got = got[:, :128] + got[:, 128:]
            P1[tick, s, n % 2] = got.reshape(2, 4, 4, 8, 128)
            return carry

        lax.fori_loop(0, 8, one, 0, unroll=2)

    def spread(tick, s, slabs, near, far, sems, stride, pos):
        over = (pos + 2) % 4
        (near_send, near_recv), (far_send, far_recv) = sems

        @pl.when(tick < TICKS - DIRECT)
        def _():
            for half, hop in ((0, 1), (1, 3)):
                send(slabs(over).at[:, half], far.at[tick, s, :, half], far_send, far_recv, along(stride, hop))

        @pl.when(tick >= TICKS - DIRECT)
        def _():
            send(slabs(over), far.at[tick, s], far_send, far_recv, along(stride, 2))
            for slot, hop in ((0, 1), (1, 3)):
                send(slabs((pos + hop) % 4), near.at[tick, s, slot], near_send, near_recv, along(stride, hop))

    def relay(tick, s, slabs, near, far, sems, stride, pos):
        near_send, near_recv = sems
        for slot, hop in ((0, 1), (1, 3)):
            slab = slabs((pos + hop) % 4)
            slab[:, slot] += far[tick, s, :, slot]
            send(slab, near.at[tick, s, slot], near_send, near_recv, along(stride, hop))

    def slabs_of(tick, s):
        return lambda q: P1.at[tick, s, :, :, q]

    def parts_of(tick, s, a):
        return lambda q: P1.at[tick, s, :, :, a, q]

    def first_send(tick):
        sems = ((s2.at[tick], r2.at[tick]), (s1.at[tick], r1.at[tick]))
        for s in range(STREAMS):
            spread(tick, s, slabs_of(tick, s), R2, R1, sems, *axis_of(order_of(s, tick), 0))

    def first_pass(tick):
        wait(R1.at[tick], r1.at[tick])

        @pl.when(tick < TICKS - DIRECT)
        def _():
            for s in range(STREAMS):
                sems = (s2.at[tick], r2.at[tick])
                relay(tick, s, slabs_of(tick, s), R2, R1, sems, *axis_of(order_of(s, tick), 0))

    def second_send(tick):
        wait(R2.at[tick], r2.at[tick])
        sems = ((s4.at[tick], r4.at[tick]), (s3.at[tick], r3.at[tick]))
        for s in range(STREAMS):
            _, a = axis_of(order_of(s, tick), 0)
            P1[tick, s, :, :, a] += R2[tick, s, 0] + R2[tick, s, 1]

            @pl.when(tick >= TICKS - DIRECT)
            def _():
                P1[tick, s, :, :, a] += R1[tick, s]

            spread(tick, s, parts_of(tick, s, a), R4, R3, sems, *axis_of(order_of(s, tick), 1))

    def second_pass(tick):
        wait(R3.at[tick], r3.at[tick])

        @pl.when(tick < TICKS - DIRECT)
        def _():
            for s in range(STREAMS):
                _, a = axis_of(order_of(s, tick), 0)
                sems = (s4.at[tick], r4.at[tick])
                relay(tick, s, parts_of(tick, s, a), R4, R3, sems, *axis_of(order_of(s, tick), 1))

    def third_send(tick):
        wait(R4.at[tick], r4.at[tick])
        for s in range(STREAMS):
            _, a = axis_of(order_of(s, tick), 0)
            _, b = axis_of(order_of(s, tick), 1)

            @pl.when(tick >= TICKS - DIRECT)
            def _():
                P1[tick, s, :, :, a, b] += R3[tick, s]

            total = P1[tick, s, :, :, a, b] + R4[tick, s, 0] + R4[tick, s, 1]
            for g in range(2):
                for j in range(2):
                    for q in range(4):
                        for ct in range(2):
                            row = ct * 4 + g * 2 + j
                            T3[tick, s, q, row : row + 1, :] = total[g, j, 2 * q + ct : 2 * q + ct + 1, :]
            stride, d = axis_of(order_of(s, tick), 2)
            for hop in (1, 2, 3):
                send(
                    T3.at[tick, s, (d + hop) % 4], R5.at[tick, s, hop - 1], s5.at[tick], r5.at[tick],
                    along(stride, hop),
                )

    scale = 1.0 / math.sqrt(ROWS)

    def last(tick):
        wait(R5.at[tick], r5.at[tick])
        done = []
        for s in range(STREAMS):
            _, d = axis_of(order_of(s, tick), 2)
            done.append((T3[tick, s, d] + R5[tick, s, 0] + R5[tick, s, 1] + R5[tick, s, 2]) * scale)
        for ct in range(2):
            for pair in range(2):
                rows = pl.ds(pl.multiple_of(tick * 16 + pair * 8, 8), 8)
                WF[ct, rows, :] = jnp.concatenate(
                    [done[2 * pair][4 * ct : 4 * ct + 4], done[2 * pair + 1][4 * ct : 4 * ct + 4]], axis=0
                )

    def tick_step(i, carry):
        @pl.when(i < TICKS)
        def _():
            wait(SIB.at[i], sib_recv.at[i])
            produce(i)
            first_send(i)

        for n, work in enumerate((first_pass, second_send, second_pass, third_send, last), 1):
            lag = n * LAG

            @pl.when((i >= lag) & (i < TICKS + lag))
            def _():
                work(i - lag)

        return carry

    lax.fori_loop(0, TICKS + 5 * LAG, tick_step, 0)

    send(WF.at[1 - core], WALL.at[core], w_send, w_recv, sibling)
    high, mid, low = split3(WF[...].reshape(256, 128))
    square = dot_tt(high, jnp.concatenate([high, mid], axis=1))
    rest = dot_tt(mid, jnp.concatenate([mid, low], axis=1))
    outer = dot_tt(high, low)
    cross = square[:, 128:] + outer
    gram = square[:, :128] + rest[:, :128] + (cross + cross.T)
    G[...] = (gram * (1.0 / SAMP_OWN)).reshape(2, 64, 128)
    send(G.at[1 - core], RG1, g1_send, g1_recv, sibling)
    wait(RG1, g1_recv)
    G[core] += RG1[...]
    for hop in (1, 2, 3):
        send(G.at[core], RG2.at[hop - 1], g2_send.at[hop - 1], g2_recv.at[hop - 1], along(2, hop))

    WALL[core] = WF[core]
    wait(WALL.at[0], w_recv)
    back = jnp.where(iota((256, 256), 0) == POS[...], 1.0, 0.0).astype(BF16)
    sketch_ref[...] = sum(dot_tt(back, term) for term in split3(WALL[...].reshape(256, 128)))

    for hop in (1, 2, 3):
        wait(RG2.at[0], g2_recv.at[hop - 1])
    terms = [G[core], RG2[0], RG2[1], RG2[2]]
    GF[core] = (terms[0] + terms[2]) + (terms[1] + terms[3])
    send(GF.at[core], GF.at[core], g3_send, g3_recv, sibling)
    wait(GF.at[0], g3_recv)

    sub16 = iota((16, 128), 0)
    lane16 = iota((16, 128), 1)
    work = GF[...].reshape(128, 128)
    for r in range(8):
        panel = work[:16]
        columns = [jnp.broadcast_to(panel[:, 16 * r + k : 16 * r + k + 1], (16, 128)) for k in range(16)]
        scales = jnp.zeros((16, 128), F32)
        for j in range(16):
            inverse = lax.rsqrt(columns[j][j : j + 1])
            square = inverse * inverse
            below = jnp.where(sub16 > j, columns[j], 0.0)
            scales = jnp.where(sub16 == j, inverse, scales)
            for k in range(j + 1, 16):
                columns[k] = columns[k] - (below * columns[k][j : j + 1]) * square
            panel = panel - (below * panel[j : j + 1]) * square
        panel = jnp.where(lane16 >= 16 * r + sub16, panel * scales, 0.0)

        @pl.when(core == r % 2)
        def _():
            OUT[z_pos, x_pos, r] = panel
            block = OUT.at[z_pos, x_pos, r]
            for dz, dx in plane:
                send(block, block, o_send.at[r // 2], o_recv.at[r // 2], peer(dz, dx))

        if r < 7:
            h, m, l = (term.astype(F32) for term in split3(panel))
            lhs = jnp.concatenate([h, h, m, m, h, l], axis=0).astype(BF16)
            rhs = jnp.concatenate([h, m, h, m, l, h], axis=0).astype(BF16)
            work = work[16:] - dot_tt(lhs, rhs)[16 * r + 16 :]

    def share(n):
        slab = OUT.at[:, :, 2 * n + core]
        wait(DUM, o_recv.at[n])
        send(slab, slab, f_send.at[n], f_recv.at[n], sibling)
        return pltpu.make_async_copy(slab, factors_ref.at[:, :, 2 * n + core], out_sem.at[n])

    def store(n):
        return pltpu.make_async_copy(
            OUT.at[:, :, 2 * n + 1 - core], factors_ref.at[:, :, 2 * n + 1 - core], out_sem.at[4 + n]
        )

    for n in range(4):
        share(n).start()
    for n in range(4):
        wait(OUT.at[:, :, 0], f_recv.at[n])
        store(n).start()

    for n in range(7):
        wait(Y8.at[0], y_send.at[n])
    wait(DUM, p_send)
    for n in range(3):
        wait(RG2.at[0], g2_send.at[n])
    for n in range(4):
        wait(DUM, o_send.at[n])
        wait(OUT.at[:, :, 0], f_send.at[n])
    wait(GF.at[0], g3_send)
    wait(RG1, g1_send)
    wait(WALL.at[0], w_send)

    def sent(tick, carry):
        wait(SIB.at[tick], sib_send.at[tick])
        wait(R1.at[tick], s1.at[tick])
        wait(R2.at[tick], s2.at[tick])
        wait(R3.at[tick], s3.at[tick])
        wait(R4.at[tick], s4.at[tick])
        wait(R5.at[tick], s5.at[tick])
        return carry

    lax.fori_loop(0, TICKS, sent, 0)
    for n in range(8):
        wait(OUT.at[:, :, 0], out_sem.at[n])


def body(matrix, signs, samples):
    dma = pltpu.SemaphoreType.DMA
    vmem = pltpu.VMEM
    t, s = TICKS, STREAMS
    sketch, factors = pl.pallas_call(
        kernel,
        out_shape=(
            jax.ShapeDtypeStruct((256, 128), F32),
            jax.ShapeDtypeStruct((4, 4, 8, 16, 128), F32),
        ),
        in_specs=[pl.BlockSpec(memory_space=pl.ANY)] * 3,
        out_specs=(pl.BlockSpec(memory_space=pltpu.VMEM), pl.BlockSpec(memory_space=pl.ANY)),
        scratch_shapes=[
            vmem((16, 8, 128, 128), F32),
            vmem((8, 8, 128, 128), F32),
            vmem((t, s, 2, 2, 4, 4, 8, 128), F32),
            vmem((t, s, 2, 2, 4, 8, 128), F32),
            vmem((t, s, 2, 2, 2, 4, 8, 128), F32),
            vmem((t, s, 2, 2, 8, 128), F32),
            vmem((t, s, 2, 2, 2, 8, 128), F32),
            vmem((t, s, 4, 8, 128), F32),
            vmem((t, s, 3, 8, 128), F32),
            vmem((8, 8, 128), I32),
            vmem((4, 4, 2, 8, 128), I32),
            vmem((128, 128), I32),
            vmem((2, 128), I32),
            vmem((3, 2, 128, 128), I32),
            vmem((3, 2, 128, 128), F32),
            vmem((3, 2, 128, 128), F32),
            vmem((1, 256), I32),
            vmem((2, 128, 128), F32),
            vmem((2, 128, 128), F32),
            vmem((2, 64, 128), F32),
            vmem((64, 128), F32),
            vmem((3, 64, 128), F32),
            vmem((2, 64, 128), F32),
            vmem((4, 4, 8, 16, 128), F32),
            vmem((15, 16, 128), F32),
            dma((16,)), dma((2,)), dma((7,)), dma((7,)), dma(()), dma(()),
            dma((t,)), dma((t,)),
            dma((t,)), dma((t,)), dma((t,)), dma((t,)), dma((t,)), dma((t,)), dma((t,)), dma((t,)),
            dma((t,)), dma((t,)),
            dma(()), dma(()), dma(()), dma(()), dma((3,)), dma((3,)), dma(()), dma(()),
            dma((4,)), dma((4,)), dma((4,)), dma((4,)), dma((8,)),
        ],
        compiler_params=pltpu.CompilerParams(
            collective_id=0, has_side_effects=True, vmem_limit_bytes=48 * 1024 * 1024
        ),
    )(matrix.reshape(16, 8, 128, 128), signs.reshape(128, 128), samples.reshape(2, 128))
    return sketch, factors.reshape(16, 128, 128)


def solution(mesh):
    return jax.shard_map(
        body,
        mesh=mesh,
        in_specs=(P("rows", None), P("rows"), P("rows")),
        out_specs=(P("rows", None), P()),
        check_vma=False,
    )
```

```python
import functools
import math

import jax
import jax.numpy as jnp
from jax import lax
from jax.experimental import pallas as pl
from jax.experimental.pallas import tpu as pltpu
from jax.sharding import PartitionSpec as P

MESH = pl.DeviceIdType.MESH
F32 = jnp.float32
BF16 = jnp.bfloat16
I32 = jnp.int32

TICKS = 8
STREAMS = 4
ROWS = 2097152
SAMP_OWN = 2048


def dot_tt(lhs, rhs, precision=None):
    return lax.dot_general(
        lhs, rhs, (((0,), (0,)), ((), ())), precision=precision, preferred_element_type=F32
    )


def iota(shape, dim):
    return lax.broadcasted_iota(I32, shape, dim)


def odd(bits):
    bits = bits ^ (bits >> 4)
    bits = bits ^ (bits >> 2)
    bits = bits ^ (bits >> 1)
    return bits & 1


def split2(value):
    high = value.astype(BF16)
    return high, (value - high.astype(F32)).astype(BF16)


def split3(value):
    high = value.astype(BF16)
    rest = value - high.astype(F32)
    mid = rest.astype(BF16)
    return high, mid, (rest - mid.astype(F32)).astype(BF16)


def kernel(
    matrix_ref, signs_ref, samples_ref, sketch_ref, factors_ref,
    X, SIB, P1, R1, R2, R3, R4, T3, R5, Y8, IDX, SGN, SMP, ML, SO, SS, POS, WF, WALL, G, RG1, RG2, GF, OUT, DUM,
    load_sem, in_sem, y_send, y_recv, p_send, p_recv, sib_send, sib_recv,
    s1, r1, s2, r2, s3, r3, s4, r4, s5, r5,
    w_send, w_recv, g1_send, g1_recv, g2_send, g2_recv, g3_send, g3_recv,
    o_send, o_recv, f_send, f_recv, out_sem,
):
    me = lax.axis_index("rows")
    core = me % 2
    y_pos = (me // 2) % 4
    x_pos = (me // 8) % 4
    z_pos = me // 32
    sibling = me + 1 - 2 * core

    def along(stride, hop):
        pos = (me // stride) % 4
        return me + ((pos + hop) % 4 - pos) * stride

    def axis_of(order, stage):
        k = (order + stage) % 3
        stride = 32 - 33 * k + 9 * k * k
        return stride, (me // stride) % 4

    def send(src, dst, send_sem, recv_sem, device):
        copy = pltpu.make_async_remote_copy(
            src_ref=src, dst_ref=dst, send_sem=send_sem, recv_sem=recv_sem,
            device_id=(device,), device_id_type=MESH,
        )
        copy.start()

    def wait(ref, sem):
        pltpu.make_async_copy(ref, ref, sem).wait()

    def load(chunk):
        return pltpu.make_async_copy(matrix_ref.at[chunk], X.at[chunk], load_sem.at[chunk])

    fetch_samples = pltpu.make_async_copy(samples_ref, SMP, in_sem.at[0])
    fetch_samples.start()
    fetch_signs = pltpu.make_async_copy(signs_ref, SGN, in_sem.at[1])
    fetch_signs.start()
    for chunk in range(16):
        load(chunk).start()

    group = [(dy, dc) for dy in range(4) for dc in range(2) if (dy, dc) != (0, 0)]
    plane = [(dz, dx) for dz in range(4) for dx in range(4) if (dz, dx) != (0, 0)]

    def mate(dy, dc):
        return along(2, dy) + dc * (1 - 2 * core)

    def peer(dz, dx):
        return ((z_pos + dz) % 4) * 32 + ((x_pos + dx) % 4) * 8 + me % 8

    barrier = pltpu.get_barrier_semaphore()
    for dy, dc in group:
        pl.semaphore_signal(barrier, inc=1, device_id=(mate(dy, dc),), device_id_type=MESH)
    for dz, dx in plane:
        pl.semaphore_signal(barrier, inc=1, device_id=(peer(dz, dx),), device_id_type=MESH)

    had = (1 - 2 * odd(iota((128, 128), 0) & iota((128, 128), 1))).astype(F32)
    fetch_samples.wait()

    samples = SMP[...]
    part = (samples >> 7) & 127
    intervals = jnp.concatenate([part[0:1], part[1:2]], axis=1)
    values = jnp.concatenate([samples[0:1], samples[1:2]], axis=1)
    onehot = iota((128, 256), 0) == intervals
    onehot_f = jnp.where(onehot, 1.0, 0.0)
    before = jnp.where(iota((256, 256), 0) < iota((256, 256), 1), 1.0, 0.0).astype(BF16)
    count = jnp.dot(onehot_f.astype(BF16), before, preferred_element_type=F32)
    rank = jnp.sum(count * onehot_f, axis=0, keepdims=True).astype(I32)
    place = (
        (intervals >> 6) * 128 + (intervals & 7) * 16 + ((intervals >> 3) & 7) * 2 + rank
    )
    POS[...] = place
    slot = rank * 128 + intervals
    chosen = jnp.where(iota((256, 256), 0) == slot, 1.0, 0.0).astype(BF16)
    row8 = iota((8, 256), 0)
    fields = jnp.where(row8 == 0, values & 127, jnp.where(row8 == 1, values >> 14, 0))
    sorted_fields = lax.dot_general(
        fields.astype(F32).astype(BF16), chosen, (((1,), (1,)), ((), ())), preferred_element_type=F32
    ).astype(I32)
    sorted_rows = (
        sorted_fields[1:2] * 16384 + (iota((1, 256), 1) & 127) * 128 + sorted_fields[0:1]
    )
    mine8 = 2 * y_pos + core
    Y8[mine8, 0:1, :] = sorted_rows[:, :128]
    Y8[mine8, 1:2, :] = sorted_rows[:, 128:]
    def front(chunk, carry):
        load(chunk).wait()
        for al in range(8):
            high, low = split2(X[chunk, al])
            sign = SGN[pl.ds(chunk * 8 + al, 1), :].astype(F32)
            signed = (had * sign).astype(BF16)
            X[chunk, al] = jnp.dot(
                jnp.concatenate([signed, signed], axis=1),
                jnp.concatenate([high, low], axis=0),
                preferred_element_type=F32,
            )
        for tile in range(16):
            rows = slice(8 * tile, 8 * tile + 8)
            v = [X[chunk, al, rows, :] for al in range(8)]
            for span in (1, 2, 4):
                v = butterfly(v, span)
            for al in range(8):
                X[chunk, al, rows, :] = v[al]
        return carry

    def butterfly(v, span):
        out = list(v)
        for n in range(len(v)):
            if n & span == 0:
                out[n] = v[n] + v[n + span]
                out[n + span] = v[n] - v[n + span]
        return out

    fetch_signs.wait()
    lax.fori_loop(0, 4, front, 0, unroll=2)
    pl.semaphore_wait(barrier, 22)
    for n, (dy, dc) in enumerate(group):
        send(Y8.at[mine8], Y8.at[mine8], y_send.at[n], y_recv.at[n], mate(dy, dc))
    lax.fori_loop(4, 10, front, 0, unroll=2)
    for n in range(7):
        wait(Y8.at[0], y_recv.at[n])
    for q in range(8):
        for j in range(2):
            IDX[z_pos, x_pos, j, q : q + 1, :] = Y8[q, j : j + 1, :]
    for dz, dx in plane:
        send(IDX.at[z_pos, x_pos], IDX.at[z_pos, x_pos], p_send, p_recv, peer(dz, dx))
    lax.fori_loop(10, 16, front, 0, unroll=2)

    def second(step):
        def tile_step(tile, carry):
            rows = pl.ds(pl.multiple_of(tile * 8, 8), 8)
            v = [X[ah, step, rows, :] for ah in range(16)]
            for span in (1, 2, 4, 8):
                v = butterfly(v, span)
            for ah in range(16):
                X[ah, step, rows, :] = v[ah]
            return carry

        lax.fori_loop(0, 16, tile_step, 0, unroll=2)
        send(
            X.at[pl.ds((1 - core) * 8, 8), step], SIB.at[step], sib_send.at[step], sib_recv.at[step], sibling
        )

    for step in range(TICKS):
        second(step)

    wait(DUM, p_recv)
    from_t = iota((128, 128), 0)
    to_t = iota((128, 128), 1)
    hi_t, mid_t, lo_t, core_t = to_t // 32, (to_t // 8) % 4, (to_t // 2) % 4, to_t % 2
    natural = [
        hi_t * 32 + mid_t * 8 + lo_t * 2 + core_t,
        hi_t * 8 + mid_t * 2 + lo_t * 32 + core_t,
        hi_t * 2 + mid_t * 32 + lo_t * 8 + core_t,
    ]
    for order in range(3):
        perm = jnp.where(from_t == natural[order], 1.0, 0.0).astype(BF16)
        for j in range(2):
            rows = IDX[:, :, j].reshape(128, 128)
            low = (rows & 127).astype(F32).astype(BF16)
            block = (rows >> 14).astype(F32).astype(BF16)
            ML[order, j] = dot_tt(low, perm).astype(I32)
            owner = dot_tt(block, perm).astype(I32)
            SO[order, j] = (1 - 2 * odd(owner & me)).astype(F32)
            SS[order, j] = (1 - 2 * odd(owner & sibling)).astype(F32)

    sub = iota((128, 128), 0)

    def order_of(s, tick):
        return s if s < 3 else tick % 3

    def produce(tick):
        def one(n, carry):
            s = n // 2
            order = s + (s // 3) * (tick % 3 - 3)
            p = (core * 8 + n) * 8 + tick
            own_hi, own_lo = split2(X[core * 8 + n, tick])
            sib_hi, sib_lo = split2(SIB[tick, n])
            picks = []
            for j in range(2):
                hit = sub == ML[order, j, pl.ds(p, 1), :]
                own = jnp.where(hit, SO[order, j, pl.ds(p, 1), :], 0.0).astype(BF16)
                sib = jnp.where(hit, SS[order, j, pl.ds(p, 1), :], 0.0).astype(BF16)
                picks.append(jnp.concatenate([own, sib], axis=0))
            pick = jnp.concatenate(picks, axis=1)
            terms = jnp.concatenate(
                [jnp.concatenate([own_hi, sib_hi], axis=0), jnp.concatenate([own_lo, sib_lo], axis=0)], axis=1
            )
            got = dot_tt(pick, terms)
            got = got[:, :128] + got[:, 128:]
            P1[tick, s, n % 2] = got.reshape(2, 4, 4, 8, 128)
            return carry

        lax.fori_loop(0, 8, one, 0, unroll=8)

    def spread(tick, s, slabs, far, sems, stride, pos):
        over = (pos + 2) % 4
        for half, hop in ((0, 1), (1, 3)):
            send(slabs(over).at[:, half], far.at[tick, s, :, half], *sems, along(stride, hop))

    def relay(tick, s, slabs, near, far, sems, stride, pos):
        near_send, near_recv = sems
        for slot, hop in ((0, 1), (1, 3)):
            slab = slabs((pos + hop) % 4)
            slab[:, slot] += far[tick, s, :, slot]
            send(slab, near.at[tick, s, slot], near_send, near_recv, along(stride, hop))

    def slabs_of(tick, s):
        return lambda q: P1.at[tick, s, :, :, q]

    def parts_of(tick, s, a):
        return lambda q: P1.at[tick, s, :, :, a, q]

    def first_send(tick):
        for s in range(STREAMS):
            spread(tick, s, slabs_of(tick, s), R1, (s1.at[tick], r1.at[tick]), *axis_of(order_of(s, tick), 0))

    def first_pass(tick):
        wait(R1.at[tick], r1.at[tick])
        for s in range(STREAMS):
            sems = (s2.at[tick], r2.at[tick])
            relay(tick, s, slabs_of(tick, s), R2, R1, sems, *axis_of(order_of(s, tick), 0))

    def second_send(tick):
        wait(R2.at[tick], r2.at[tick])
        for s in range(STREAMS):
            _, a = axis_of(order_of(s, tick), 0)
            P1[tick, s, :, :, a] += R2[tick, s, 0] + R2[tick, s, 1]
            spread(tick, s, parts_of(tick, s, a), R3, (s3.at[tick], r3.at[tick]), *axis_of(order_of(s, tick), 1))

    def second_pass(tick):
        wait(R3.at[tick], r3.at[tick])
        for s in range(STREAMS):
            _, a = axis_of(order_of(s, tick), 0)
            sems = (s4.at[tick], r4.at[tick])
            relay(tick, s, parts_of(tick, s, a), R4, R3, sems, *axis_of(order_of(s, tick), 1))

    def third_send(tick):
        wait(R4.at[tick], r4.at[tick])
        for s in range(STREAMS):
            _, a = axis_of(order_of(s, tick), 0)
            _, b = axis_of(order_of(s, tick), 1)
            total = P1[tick, s, :, :, a, b] + R4[tick, s, 0] + R4[tick, s, 1]
            for g in range(2):
                for j in range(2):
                    for q in range(4):
                        for ct in range(2):
                            row = ct * 4 + g * 2 + j
                            T3[tick, s, q, row : row + 1, :] = total[g, j, 2 * q + ct : 2 * q + ct + 1, :]
            stride, d = axis_of(order_of(s, tick), 2)
            for hop in (1, 2, 3):
                send(
                    T3.at[tick, s, (d + hop) % 4], R5.at[tick, s, hop - 1], s5.at[tick], r5.at[tick],
                    along(stride, hop),
                )

    scale = 1.0 / math.sqrt(ROWS)

    def last(tick):
        wait(R5.at[tick], r5.at[tick])
        done = []
        for s in range(STREAMS):
            _, d = axis_of(order_of(s, tick), 2)
            done.append((T3[tick, s, d] + R5[tick, s, 0] + R5[tick, s, 1] + R5[tick, s, 2]) * scale)
        for ct in range(2):
            for pair in range(2):
                rows = pl.ds(pl.multiple_of(tick * 16 + pair * 8, 8), 8)
                WF[ct, rows, :] = jnp.concatenate(
                    [done[2 * pair][4 * ct : 4 * ct + 4], done[2 * pair + 1][4 * ct : 4 * ct + 4]], axis=0
                )

    def make(tick):
        wait(SIB.at[tick], sib_recv.at[tick])
        produce(tick)
        first_send(tick)

    def each(work):
        def step(tick, carry):
            work(tick)
            return carry

        lax.fori_loop(0, TICKS, step, 0)

    for work in (make, first_pass, second_send, second_pass, third_send, last):
        each(work)

    send(WF.at[1 - core], WALL.at[core], w_send, w_recv, sibling)
    high, mid, low = split3(WF[...].reshape(256, 128))
    square = dot_tt(high, jnp.concatenate([high, mid], axis=1))
    rest = dot_tt(mid, jnp.concatenate([mid, low], axis=1))
    outer = dot_tt(high, low)
    cross = square[:, 128:] + outer
    gram = square[:, :128] + rest[:, :128] + (cross + cross.T)
    G[...] = (gram * (1.0 / SAMP_OWN)).reshape(2, 64, 128)
    send(G.at[1 - core], RG1, g1_send, g1_recv, sibling)
    wait(RG1, g1_recv)
    G[core] += RG1[...]
    for hop in (1, 2, 3):
        send(G.at[core], RG2.at[hop - 1], g2_send.at[hop - 1], g2_recv.at[hop - 1], along(2, hop))

    WALL[core] = WF[core]
    wait(WALL.at[0], w_recv)
    back = jnp.where(iota((256, 256), 0) == POS[...], 1.0, 0.0).astype(BF16)
    sketch_ref[...] = sum(dot_tt(back, term) for term in split3(WALL[...].reshape(256, 128)))

    for hop in (1, 2, 3):
        wait(RG2.at[0], g2_recv.at[hop - 1])
    terms = [G[core], RG2[0], RG2[1], RG2[2]]
    GF[core] = (terms[0] + terms[2]) + (terms[1] + terms[3])
    send(GF.at[core], GF.at[core], g3_send, g3_recv, sibling)
    wait(GF.at[0], g3_recv)

    sub16 = iota((16, 128), 0)
    lane16 = iota((16, 128), 1)
    work = GF[...].reshape(128, 128)
    for r in range(8):
        panel = work[:16]
        columns = [jnp.broadcast_to(panel[:, 16 * r + k : 16 * r + k + 1], (16, 128)) for k in range(16)]
        scales = jnp.zeros((16, 128), F32)
        for j in range(16):
            inverse = lax.rsqrt(columns[j][j : j + 1])
            square = inverse * inverse
            below = jnp.where(sub16 > j, columns[j], 0.0)
            scales = jnp.where(sub16 == j, inverse, scales)
            for k in range(j + 1, 16):
                columns[k] = columns[k] - (below * columns[k][j : j + 1]) * square
            panel = panel - (below * panel[j : j + 1]) * square
        panel = jnp.where(lane16 >= 16 * r + sub16, panel * scales, 0.0)

        @pl.when(core == r % 2)
        def _():
            OUT[z_pos, x_pos, r] = panel
            block = OUT.at[z_pos, x_pos, r]
            for dz, dx in plane:
                send(block, block, o_send.at[r // 2], o_recv.at[r // 2], peer(dz, dx))

        if r < 7:
            h, m, l = (term.astype(F32) for term in split3(panel))
            lhs = jnp.concatenate([h, h, m, m, h, l], axis=0).astype(BF16)
            rhs = jnp.concatenate([h, m, h, m, l, h], axis=0).astype(BF16)
            work = work[16:] - dot_tt(lhs, rhs)[16 * r + 16 :]

    def share(n):
        slab = OUT.at[:, :, 2 * n + core]
        wait(DUM, o_recv.at[n])
        send(slab, slab, f_send.at[n], f_recv.at[n], sibling)
        return pltpu.make_async_copy(slab, factors_ref.at[:, :, 2 * n + core], out_sem.at[n])

    def store(n):
        return pltpu.make_async_copy(
            OUT.at[:, :, 2 * n + 1 - core], factors_ref.at[:, :, 2 * n + 1 - core], out_sem.at[4 + n]
        )

    for n in range(4):
        share(n).start()
    for n in range(4):
        wait(OUT.at[:, :, 0], f_recv.at[n])
        store(n).start()

    for n in range(7):
        wait(Y8.at[0], y_send.at[n])
    wait(DUM, p_send)
    for n in range(3):
        wait(RG2.at[0], g2_send.at[n])
    for n in range(4):
        wait(DUM, o_send.at[n])
        wait(OUT.at[:, :, 0], f_send.at[n])
    wait(GF.at[0], g3_send)
    wait(RG1, g1_send)
    wait(WALL.at[0], w_send)

    def sent(tick, carry):
        wait(SIB.at[tick], sib_send.at[tick])
        wait(R1.at[tick], s1.at[tick])
        wait(R2.at[tick], s2.at[tick])
        wait(R3.at[tick], s3.at[tick])
        wait(R4.at[tick], s4.at[tick])
        wait(R5.at[tick], s5.at[tick])
        return carry

    lax.fori_loop(0, TICKS, sent, 0)
    for n in range(8):
        wait(OUT.at[:, :, 0], out_sem.at[n])


def body(matrix, signs, samples):
    dma = pltpu.SemaphoreType.DMA
    vmem = pltpu.VMEM
    t, s = TICKS, STREAMS
    sketch, factors = pl.pallas_call(
        kernel,
        out_shape=(
            jax.ShapeDtypeStruct((256, 128), F32),
            jax.ShapeDtypeStruct((4, 4, 8, 16, 128), F32),
        ),
        in_specs=[pl.BlockSpec(memory_space=pltpu.HBM)] * 3,
        out_specs=(pl.BlockSpec(memory_space=pltpu.VMEM), pl.BlockSpec(memory_space=pl.ANY)),
        scratch_shapes=[
            vmem((16, 8, 128, 128), F32),
            vmem((8, 8, 128, 128), F32),
            vmem((t, s, 2, 2, 4, 4, 8, 128), F32),
            vmem((t, s, 2, 2, 4, 8, 128), F32),
            vmem((t, s, 2, 2, 2, 4, 8, 128), F32),
            vmem((t, s, 2, 2, 8, 128), F32),
            vmem((t, s, 2, 2, 2, 8, 128), F32),
            vmem((t, s, 4, 8, 128), F32),
            vmem((t, s, 3, 8, 128), F32),
            vmem((8, 8, 128), I32),
            vmem((4, 4, 2, 8, 128), I32),
            vmem((128, 128), I32),
            vmem((2, 128), I32),
            vmem((3, 2, 128, 128), I32),
            vmem((3, 2, 128, 128), F32),
            vmem((3, 2, 128, 128), F32),
            vmem((1, 256), I32),
            vmem((2, 128, 128), F32),
            vmem((2, 128, 128), F32),
            vmem((2, 64, 128), F32),
            vmem((64, 128), F32),
            vmem((3, 64, 128), F32),
            vmem((2, 64, 128), F32),
            vmem((4, 4, 8, 16, 128), F32),
            vmem((15, 16, 128), F32),
            dma((16,)), dma((2,)), dma((7,)), dma((7,)), dma(()), dma(()),
            dma((t,)), dma((t,)),
            dma((t,)), dma((t,)), dma((t,)), dma((t,)), dma((t,)), dma((t,)), dma((t,)), dma((t,)),
            dma((t,)), dma((t,)),
            dma(()), dma(()), dma(()), dma(()), dma((3,)), dma((3,)), dma(()), dma(()),
            dma((4,)), dma((4,)), dma((4,)), dma((4,)), dma((8,)),
        ],
        compiler_params=pltpu.CompilerParams(
            collective_id=0, has_side_effects=True, vmem_limit_bytes=48 * 1024 * 1024
        ),
    )(matrix.reshape(16, 8, 128, 128), signs.reshape(128, 128), samples.reshape(2, 128))
    return sketch, factors.reshape(16, 128, 128)


def solution(mesh):
    return jax.shard_map(
        body,
        mesh=mesh,
        in_specs=(P("rows", None), P("rows"), P("rows")),
        out_specs=(P("rows", None), P()),
        check_vma=False,
    )
```

```python
import functools
import math

import jax
import jax.numpy as jnp
from jax import lax
from jax.experimental import pallas as pl
from jax.experimental.pallas import tpu as pltpu
from jax.sharding import PartitionSpec as P

MESH = pl.DeviceIdType.MESH
F32 = jnp.float32
BF16 = jnp.bfloat16
I32 = jnp.int32

TICKS = 8
EARLY = 2
STREAMS = 4
ROWS = 2097152
SAMP_OWN = 2048


def dot_tt(lhs, rhs, precision=None):
    return lax.dot_general(
        lhs, rhs, (((0,), (0,)), ((), ())), precision=precision, preferred_element_type=F32
    )


def iota(shape, dim):
    return lax.broadcasted_iota(I32, shape, dim)


def odd(bits):
    bits = bits ^ (bits >> 4)
    bits = bits ^ (bits >> 2)
    bits = bits ^ (bits >> 1)
    return bits & 1


def split2(value):
    high = value.astype(BF16)
    return high, (value - high.astype(F32)).astype(BF16)


def split3(value):
    high = value.astype(BF16)
    rest = value - high.astype(F32)
    mid = rest.astype(BF16)
    return high, mid, (rest - mid.astype(F32)).astype(BF16)


def kernel(
    matrix_ref, signs_ref, samples_ref, sketch_ref, factors_ref,
    X, SIB, P1, R1, R2, R3, R4, T3, R5, Y8, IDX, SGN, SMP, ML, OW, EB, FT, ET, POS, WF, WALL, G, RG1, RG2, GF, OUT, DUM,
    load_sem, in_sem, y_send, y_recv, p_send, p_recv, sib_send, sib_recv,
    e_send, e_recv, x_send, x_recv, s1, r1, s2, r2, s3, r3, s4, r4, s5, r5,
    w_send, w_recv, g1_send, g1_recv, g2_send, g2_recv, g3_send, g3_recv,
    o_send, o_recv, f_send, f_recv, out_sem,
):
    me = lax.axis_index("rows")
    core = me % 2
    y_pos = (me // 2) % 4
    x_pos = (me // 8) % 4
    z_pos = me // 32
    sibling = me + 1 - 2 * core

    def along(stride, hop):
        pos = (me // stride) % 4
        return me + ((pos + hop) % 4 - pos) * stride

    def send(src, dst, send_sem, recv_sem, device):
        copy = pltpu.make_async_remote_copy(
            src_ref=src, dst_ref=dst, send_sem=send_sem, recv_sem=recv_sem,
            device_id=(device,), device_id_type=MESH,
        )
        copy.start()

    def wait(ref, sem):
        pltpu.make_async_copy(ref, ref, sem).wait()

    def load(chunk):
        return pltpu.make_async_copy(matrix_ref.at[chunk], X.at[chunk], load_sem.at[chunk])

    fetch_samples = pltpu.make_async_copy(samples_ref, SMP, in_sem.at[0])
    fetch_samples.start()
    fetch_signs = pltpu.make_async_copy(signs_ref, SGN, in_sem.at[1])
    fetch_signs.start()
    for chunk in range(16):
        load(chunk).start()

    group = [(dy, dc) for dy in range(4) for dc in range(2) if (dy, dc) != (0, 0)]
    plane = [(dz, dx) for dz in range(4) for dx in range(4) if (dz, dx) != (0, 0)]

    def mate(dy, dc):
        return along(2, dy) + dc * (1 - 2 * core)

    def peer(dz, dx):
        return ((z_pos + dz) % 4) * 32 + ((x_pos + dx) % 4) * 8 + me % 8

    barrier = pltpu.get_barrier_semaphore()
    for dy, dc in group:
        pl.semaphore_signal(barrier, inc=1, device_id=(mate(dy, dc),), device_id_type=MESH)
    for dz, dx in plane:
        pl.semaphore_signal(barrier, inc=1, device_id=(peer(dz, dx),), device_id_type=MESH)

    had = (1 - 2 * odd(iota((128, 128), 0) & iota((128, 128), 1))).astype(F32)
    fetch_samples.wait()

    samples = SMP[...]
    part = (samples >> 7) & 127
    intervals = jnp.concatenate([part[0:1], part[1:2]], axis=1)
    values = jnp.concatenate([samples[0:1], samples[1:2]], axis=1)
    onehot = iota((128, 256), 0) == intervals
    onehot_f = jnp.where(onehot, 1.0, 0.0)
    before = jnp.where(iota((256, 256), 0) < iota((256, 256), 1), 1.0, 0.0).astype(BF16)
    count = jnp.dot(onehot_f.astype(BF16), before, preferred_element_type=F32)
    rank = jnp.sum(count * onehot_f, axis=0, keepdims=True).astype(I32)
    place = (
        (intervals >> 6) * 128 + (intervals & 7) * 16 + ((intervals >> 3) & 7) * 2 + rank
    )
    POS[...] = place
    slot = rank * 128 + intervals
    chosen = jnp.where(iota((256, 256), 0) == slot, 1.0, 0.0).astype(BF16)
    row8 = iota((8, 256), 0)
    fields = jnp.where(row8 == 0, values & 127, jnp.where(row8 == 1, values >> 14, 0))
    sorted_fields = lax.dot_general(
        fields.astype(F32).astype(BF16), chosen, (((1,), (1,)), ((), ())), preferred_element_type=F32
    ).astype(I32)
    sorted_rows = (
        sorted_fields[1:2] * 16384 + (iota((1, 256), 1) & 127) * 128 + sorted_fields[0:1]
    )
    mine8 = 2 * y_pos + core
    Y8[mine8, 0:1, :] = sorted_rows[:, :128]
    Y8[mine8, 1:2, :] = sorted_rows[:, 128:]
    def front(chunk, carry):
        load(chunk).wait()
        for al in range(8):
            high, low = split2(X[chunk, al])
            sign = SGN[pl.ds(chunk * 8 + al, 1), :].astype(F32)
            signed = (had * sign).astype(BF16)
            X[chunk, al] = jnp.dot(
                jnp.concatenate([signed, signed], axis=1),
                jnp.concatenate([high, low], axis=0),
                preferred_element_type=F32,
            )
        for tile in range(16):
            rows = slice(8 * tile, 8 * tile + 8)
            v = [X[chunk, al, rows, :] for al in range(8)]
            for span in (1, 2, 4):
                v = butterfly(v, span)
            for al in range(8):
                X[chunk, al, rows, :] = v[al]
        return carry

    def butterfly(v, span):
        out = list(v)
        for n in range(len(v)):
            if n & span == 0:
                out[n] = v[n] + v[n + span]
                out[n + span] = v[n] - v[n + span]
        return out

    fetch_signs.wait()
    lax.fori_loop(0, 4, front, 0, unroll=2)
    pl.semaphore_wait(barrier, 22)
    for n, (dy, dc) in enumerate(group):
        send(Y8.at[mine8], Y8.at[mine8], y_send.at[n], y_recv.at[n], mate(dy, dc))
    lax.fori_loop(4, 10, front, 0, unroll=2)
    for n in range(7):
        wait(Y8.at[0], y_recv.at[n])
    for q in range(8):
        for j in range(2):
            IDX[z_pos, x_pos, j, q : q + 1, :] = Y8[q, j : j + 1, :]
    for dz, dx in plane:
        send(IDX.at[z_pos, x_pos], IDX.at[z_pos, x_pos], p_send, p_recv, peer(dz, dx))
    lax.fori_loop(10, 16, front, 0, unroll=2)

    def second(step):
        def tile_step(tile, carry):
            rows = pl.ds(pl.multiple_of(tile * 8, 8), 8)
            v = [X[ah, step, rows, :] for ah in range(16)]
            for span in (1, 2, 4, 8):
                v = butterfly(v, span)
            for ah in range(16):
                X[ah, step, rows, :] = v[ah]
            return carry

        lax.fori_loop(0, 16, tile_step, 0, unroll=2)
        send(
            X.at[pl.ds((1 - core) * 8, 8), step], SIB.at[step], sib_send.at[step], sib_recv.at[step], sibling
        )

    def axis_of(order, stage):
        k = (order + stage) % 3
        stride = 32 - 33 * k + 9 * k * k
        return stride, (me // stride) % 4

    def block_of(s, q, sib):
        return SIB.at[q // 2, 2 * s + q % 2] if sib else X.at[core * 8 + 2 * s + q % 2, q // 2]

    def early_send(sib):
        for s in range(3):
            stride, a = axis_of(s, 0)
            for hop in (1, 2, 3):
                send(
                    block_of(s, (a + hop) % 4, sib), EB.at[s, a, sib], e_send.at[s], e_recv.at[s],
                    along(stride, hop),
                )

    second(0)
    second(1)
    early_send(0)
    second(2)
    second(3)
    wait(SIB.at[0], sib_recv.at[0])
    wait(SIB.at[1], sib_recv.at[1])
    early_send(1)
    for s in range(3):
        _, a = axis_of(s, 0)
        for sib in (0, 1):
            EB[s, a, sib] = block_of(s, a, sib)[...]
    for step in range(4, TICKS):
        second(step)

    wait(DUM, p_recv)
    from_t = iota((128, 128), 0)
    to_t = iota((128, 128), 1)
    hi_t, mid_t, lo_t, core_t = to_t // 32, (to_t // 8) % 4, (to_t // 2) % 4, to_t % 2
    natural = [
        hi_t * 32 + mid_t * 8 + lo_t * 2 + core_t,
        hi_t * 8 + mid_t * 2 + lo_t * 32 + core_t,
        hi_t * 2 + mid_t * 32 + lo_t * 8 + core_t,
    ]
    for order in range(3):
        perm = jnp.where(from_t == natural[order], 1.0, 0.0).astype(BF16)
        for j in range(2):
            rows = IDX[:, :, j].reshape(128, 128)
            low = (rows & 127).astype(F32).astype(BF16)
            block = (rows >> 14).astype(F32).astype(BF16)
            ML[order, j] = dot_tt(low, perm).astype(I32)
            OW[order, j] = dot_tt(block, perm).astype(I32)

    sub = iota((128, 128), 0)

    def order_of(s, tick):
        return s if s < 3 else tick % 3

    def picked(order, p, device, own, sib):
        picks = []
        for j in range(2):
            hit = sub == ML[order, j, pl.ds(p, 1), :]
            owner = OW[order, j, pl.ds(p, 1), :]
            for bits in (owner & device, owner & (device + 1 - 2 * core)):
                picks.append(jnp.where(hit, (1 - 2 * odd(bits)).astype(F32), 0.0).astype(BF16))
        pick = jnp.concatenate(
            [jnp.concatenate(picks[:2], axis=0), jnp.concatenate(picks[2:], axis=0)], axis=1
        )
        own_hi, own_lo = split2(own)
        sib_hi, sib_lo = split2(sib)
        terms = jnp.concatenate(
            [jnp.concatenate([own_hi, sib_hi], axis=0), jnp.concatenate([own_lo, sib_lo], axis=0)], axis=1
        )
        got = dot_tt(pick, terms)
        return got[:, :128] + got[:, 128:]

    def produce(tick, first):
        def one(n, carry):
            s = n // 2
            order = s + (s // 3) * (tick % 3 - 3)
            p = (core * 8 + n) * 8 + tick
            got = picked(order, p, me, X[core * 8 + n, tick], SIB[tick, n])
            P1[tick, s, n % 2] = got.reshape(2, 4, 4, 8, 128)
            return carry

        lax.fori_loop(first, 8, one, 0, unroll=8 - first)

    def produce_early(s, carry):
        stride, a = axis_of(s, 0)
        p = (core * 8 + 2 * s + a % 2) * 8 + a // 2
        wait(EB.at[0, pl.ds(0, 3)], e_recv.at[s])
        got = sum(picked(s, p, me + (q - a) * stride, EB[s, q, 0], EB[s, q, 1]) for q in range(4))
        got = got.reshape(2, 4, 4, 8, 128)
        for q in range(4):
            for j in range(2):
                P1[q // 2, s, q % 2, j, a] = got[j, q]
        return carry

    def spread(tick, s, slabs, far, sems, stride, pos):
        over = (pos + 2) % 4
        for half, hop in ((0, 1), (1, 3)):
            send(slabs(over).at[:, half], far.at[tick, s, :, half], *sems, along(stride, hop))

    def relay(tick, s, slabs, near, far, sems, stride, pos):
        near_send, near_recv = sems
        for slot, hop in ((0, 1), (1, 3)):
            slab = slabs((pos + hop) % 4)
            slab[:, slot] += far[tick, s, :, slot]
            send(slab, near.at[tick, s, slot], near_send, near_recv, along(stride, hop))

    def slabs_of(tick, s):
        return lambda q: P1.at[tick, s, :, :, q]

    def parts_of(tick, s, a):
        return lambda q: P1.at[tick, s, :, :, a, q]

    def wait_streams(ref, sem, tick, streams):
        wait(ref.at[tick] if len(streams) == STREAMS else ref.at[tick, 3], sem.at[tick])

    def first_send(tick, streams):
        for s in streams:
            spread(tick, s, slabs_of(tick, s), R1, (s1.at[tick], r1.at[tick]), *axis_of(order_of(s, tick), 0))

    def first_pass(tick, streams):
        wait_streams(R1, r1, tick, streams)
        for s in streams:
            sems = (s2.at[tick], r2.at[tick])
            relay(tick, s, slabs_of(tick, s), R2, R1, sems, *axis_of(order_of(s, tick), 0))

    def second_send(tick, streams):
        wait_streams(R2, r2, tick, streams)
        for s in range(STREAMS):
            _, a = axis_of(order_of(s, tick), 0)
            if s in streams:
                P1[tick, s, :, :, a] += R2[tick, s, 0] + R2[tick, s, 1]
            spread(tick, s, parts_of(tick, s, a), R3, (s3.at[tick], r3.at[tick]), *axis_of(order_of(s, tick), 1))

    def second_pass(tick, streams):
        wait(R3.at[tick], r3.at[tick])
        for s in range(STREAMS):
            _, a = axis_of(order_of(s, tick), 0)
            sems = (s4.at[tick], r4.at[tick])
            relay(tick, s, parts_of(tick, s, a), R4, R3, sems, *axis_of(order_of(s, tick), 1))

    def third_send(tick, streams):
        wait(R4.at[tick], r4.at[tick])
        for s in range(STREAMS):
            _, a = axis_of(order_of(s, tick), 0)
            _, b = axis_of(order_of(s, tick), 1)
            total = P1[tick, s, :, :, a, b] + R4[tick, s, 0] + R4[tick, s, 1]
            for g in range(2):
                for j in range(2):
                    for q in range(4):
                        for ct in range(2):
                            row = ct * 4 + g * 2 + j
                            T3[tick, s, q, row : row + 1, :] = total[g, j, 2 * q + ct : 2 * q + ct + 1, :]
            stride, d = axis_of(order_of(s, tick), 2)
            for hop in (1, 2, 3):
                send(
                    T3.at[tick, s, (d + hop) % 4], R5.at[tick, s, hop - 1], s5.at[tick], r5.at[tick],
                    along(stride, hop),
                )

    scale = 1.0 / math.sqrt(ROWS)

    def last(tick, streams):
        wait(R5.at[tick], r5.at[tick])
        done = []
        for s in range(STREAMS):
            _, d = axis_of(order_of(s, tick), 2)
            done.append((T3[tick, s, d] + R5[tick, s, 0] + R5[tick, s, 1] + R5[tick, s, 2]) * scale)
            if s not in streams:
                FT[tick, s] = done[s]
        if len(streams) < STREAMS:
            for ct in range(2):
                WF[ct, pl.ds(pl.multiple_of(tick * 16 + 8, 8), 8), :] = jnp.concatenate(
                    [done[3][4 * ct : 4 * ct + 4]] * 2, axis=0
                )
            return
        for ct in range(2):
            for pair in range(2):
                rows = pl.ds(pl.multiple_of(tick * 16 + pair * 8, 8), 8)
                WF[ct, rows, :] = jnp.concatenate(
                    [done[2 * pair][4 * ct : 4 * ct + 4], done[2 * pair + 1][4 * ct : 4 * ct + 4]], axis=0
                )

    def make(tick, streams):
        if len(streams) == STREAMS:
            wait(SIB.at[tick], sib_recv.at[tick])
        produce(tick, 2 * streams[0])
        first_send(tick, streams)

    everything, late = (0, 1, 2, 3), (3,)

    def each(work, start, stop, streams):
        def step(tick, carry):
            work(tick, streams)
            return carry

        lax.fori_loop(start, stop, step, 0)

    for work in (make, first_pass, second_send, second_pass, third_send, last):
        each(work, 0, EARLY, late)
        if work is last:
            for s in range(3):
                stride, a = axis_of(s, 0)
                for hop in (1, 2, 3):
                    send(FT.at[((a + hop) % 4) // 2, s], ET.at[s, a], x_send.at[s], x_recv.at[s], along(stride, hop))
                ET[s, a] = FT[a // 2, s]
        each(work, EARLY, TICKS, everything)
        if work is make:
            lax.fori_loop(0, 3, produce_early, 0)

    for s in range(3):
        wait(ET.at[0, pl.ds(0, 3)], x_recv.at[s])
    for tick in range(EARLY):
        for ct in range(2):
            rows = []
            for s in range(3):
                _, a = axis_of(s, 0)
                for g in range(2):
                    tile = ET[s, 2 * tick + g]
                    pair = [tile[4 * ct + 2 * n : 4 * ct + 2 * n + 2] for n in range(2)]
                    rows.append(jnp.where(a % 2 == 0, pair[0], pair[1]))
            rows.append(WF[ct, 16 * tick + 12 : 16 * tick + 16, :])
            WF[ct, 16 * tick : 16 * tick + 16, :] = jnp.concatenate(rows, axis=0)

    send(WF.at[1 - core], WALL.at[core], w_send, w_recv, sibling)
    high, mid, low = split3(WF[...].reshape(256, 128))
    square = dot_tt(high, jnp.concatenate([high, mid], axis=1))
    rest = dot_tt(mid, jnp.concatenate([mid, low], axis=1))
    outer = dot_tt(high, low)
    cross = square[:, 128:] + outer
    gram = square[:, :128] + rest[:, :128] + (cross + cross.T)
    G[...] = (gram * (1.0 / SAMP_OWN)).reshape(2, 64, 128)
    send(G.at[1 - core], RG1, g1_send, g1_recv, sibling)
    wait(RG1, g1_recv)
    G[core] += RG1[...]
    for hop in (1, 2, 3):
        send(G.at[core], RG2.at[hop - 1], g2_send.at[hop - 1], g2_recv.at[hop - 1], along(2, hop))

    WALL[core] = WF[core]
    wait(WALL.at[0], w_recv)
    back = jnp.where(iota((256, 256), 0) == POS[...], 1.0, 0.0).astype(BF16)
    sketch_ref[...] = sum(dot_tt(back, term) for term in split3(WALL[...].reshape(256, 128)))

    for hop in (1, 2, 3):
        wait(RG2.at[0], g2_recv.at[hop - 1])
    terms = [G[core], RG2[0], RG2[1], RG2[2]]
    GF[core] = (terms[0] + terms[2]) + (terms[1] + terms[3])
    send(GF.at[core], GF.at[core], g3_send, g3_recv, sibling)
    wait(GF.at[0], g3_recv)

    sub16 = iota((16, 128), 0)
    lane16 = iota((16, 128), 1)
    work = GF[...].reshape(128, 128)
    for r in range(8):
        panel = work[:16]
        columns = [jnp.broadcast_to(panel[:, 16 * r + k : 16 * r + k + 1], (16, 128)) for k in range(16)]
        scales = jnp.zeros((16, 128), F32)
        for j in range(16):
            inverse = lax.rsqrt(columns[j][j : j + 1])
            square = inverse * inverse
            below = jnp.where(sub16 > j, columns[j], 0.0)
            scales = jnp.where(sub16 == j, inverse, scales)
            for k in range(j + 1, 16):
                columns[k] = columns[k] - (below * columns[k][j : j + 1]) * square
            panel = panel - (below * panel[j : j + 1]) * square
        panel = jnp.where(lane16 >= 16 * r + sub16, panel * scales, 0.0)

        @pl.when(core == r % 2)
        def _():
            OUT[z_pos, x_pos, r] = panel
            block = OUT.at[z_pos, x_pos, r]
            for dz, dx in plane:
                send(block, block, o_send.at[r // 2], o_recv.at[r // 2], peer(dz, dx))

        if r < 7:
            h, m, l = (term.astype(F32) for term in split3(panel))
            lhs = jnp.concatenate([h, h, m, m, h, l], axis=0).astype(BF16)
            rhs = jnp.concatenate([h, m, h, m, l, h], axis=0).astype(BF16)
            work = work[16:] - dot_tt(lhs, rhs)[16 * r + 16 :]

    def share(n):
        slab = OUT.at[:, :, 2 * n + core]
        wait(DUM, o_recv.at[n])
        send(slab, slab, f_send.at[n], f_recv.at[n], sibling)
        return pltpu.make_async_copy(slab, factors_ref.at[:, :, 2 * n + core], out_sem.at[n])

    def store(n):
        return pltpu.make_async_copy(
            OUT.at[:, :, 2 * n + 1 - core], factors_ref.at[:, :, 2 * n + 1 - core], out_sem.at[4 + n]
        )

    for n in range(4):
        share(n).start()
    for n in range(4):
        wait(OUT.at[:, :, 0], f_recv.at[n])
        store(n).start()

    for n in range(7):
        wait(Y8.at[0], y_send.at[n])
    wait(DUM, p_send)
    for n in range(3):
        wait(RG2.at[0], g2_send.at[n])
    for n in range(4):
        wait(DUM, o_send.at[n])
        wait(OUT.at[:, :, 0], f_send.at[n])
    wait(GF.at[0], g3_send)
    wait(RG1, g1_send)
    wait(WALL.at[0], w_send)

    for s in range(3):
        wait(EB.at[0, pl.ds(0, 3)], e_send.at[s])
        wait(ET.at[0, pl.ds(0, 3)], x_send.at[s])

    def sent(tick, streams):
        wait(SIB.at[tick], sib_send.at[tick])
        wait_streams(R1, s1, tick, streams)
        wait_streams(R2, s2, tick, streams)
        wait(R3.at[tick], s3.at[tick])
        wait(R4.at[tick], s4.at[tick])
        wait(R5.at[tick], s5.at[tick])

    each(sent, 0, EARLY, late)
    each(sent, EARLY, TICKS, everything)
    for n in range(8):
        wait(OUT.at[:, :, 0], out_sem.at[n])


def body(matrix, signs, samples):
    dma = pltpu.SemaphoreType.DMA
    vmem = pltpu.VMEM
    t, s = TICKS, STREAMS
    sketch, factors = pl.pallas_call(
        kernel,
        out_shape=(
            jax.ShapeDtypeStruct((256, 128), F32),
            jax.ShapeDtypeStruct((4, 4, 8, 16, 128), F32),
        ),
        in_specs=[pl.BlockSpec(memory_space=pltpu.HBM)] * 3,
        out_specs=(pl.BlockSpec(memory_space=pltpu.VMEM), pl.BlockSpec(memory_space=pl.ANY)),
        scratch_shapes=[
            vmem((16, 8, 128, 128), F32),
            vmem((8, 8, 128, 128), F32),
            vmem((t, s, 2, 2, 4, 4, 8, 128), F32),
            vmem((t, s, 2, 2, 4, 8, 128), F32),
            vmem((t, s, 2, 2, 2, 4, 8, 128), F32),
            vmem((t, s, 2, 2, 8, 128), F32),
            vmem((t, s, 2, 2, 2, 8, 128), F32),
            vmem((t, s, 4, 8, 128), F32),
            vmem((t, s, 3, 8, 128), F32),
            vmem((8, 8, 128), I32),
            vmem((4, 4, 2, 8, 128), I32),
            vmem((128, 128), I32),
            vmem((2, 128), I32),
            vmem((3, 2, 128, 128), I32),
            vmem((3, 2, 128, 128), I32),
            vmem((3, 4, 2, 128, 128), F32),
            vmem((2, 3, 8, 128), F32),
            vmem((3, 4, 8, 128), F32),
            vmem((1, 256), I32),
            vmem((2, 128, 128), F32),
            vmem((2, 128, 128), F32),
            vmem((2, 64, 128), F32),
            vmem((64, 128), F32),
            vmem((3, 64, 128), F32),
            vmem((2, 64, 128), F32),
            vmem((4, 4, 8, 16, 128), F32),
            vmem((15, 16, 128), F32),
            dma((16,)), dma((2,)), dma((7,)), dma((7,)), dma(()), dma(()),
            dma((t,)), dma((t,)),
            dma((3,)), dma((3,)), dma((3,)), dma((3,)),
            dma((t,)), dma((t,)), dma((t,)), dma((t,)), dma((t,)), dma((t,)), dma((t,)), dma((t,)),
            dma((t,)), dma((t,)),
            dma(()), dma(()), dma(()), dma(()), dma((3,)), dma((3,)), dma(()), dma(()),
            dma((4,)), dma((4,)), dma((4,)), dma((4,)), dma((8,)),
        ],
        compiler_params=pltpu.CompilerParams(
            collective_id=0, has_side_effects=True, vmem_limit_bytes=48 * 1024 * 1024
        ),
    )(matrix.reshape(16, 8, 128, 128), signs.reshape(128, 128), samples.reshape(2, 128))
    return sketch, factors.reshape(16, 128, 128)


def solution(mesh):
    return jax.shard_map(
        body,
        mesh=mesh,
        in_specs=(P("rows", None), P("rows"), P("rows")),
        out_specs=(P("rows", None), P()),
        check_vma=False,
    )
```

```python
import functools
import math

import jax
import jax.numpy as jnp
from jax import lax
from jax.experimental import pallas as pl
from jax.experimental.pallas import tpu as pltpu
from jax.sharding import PartitionSpec as P

MESH = pl.DeviceIdType.MESH
F32 = jnp.float32
BF16 = jnp.bfloat16
I32 = jnp.int32

TICKS = 8
EARLY = 2
STREAMS = 4
ROWS = 2097152
SAMP_OWN = 2048


def dot_tt(lhs, rhs, precision=None):
    return lax.dot_general(
        lhs, rhs, (((0,), (0,)), ((), ())), precision=precision, preferred_element_type=F32
    )


def iota(shape, dim):
    return lax.broadcasted_iota(I32, shape, dim)


def odd(bits):
    bits = bits ^ (bits >> 4)
    bits = bits ^ (bits >> 2)
    bits = bits ^ (bits >> 1)
    return bits & 1


def split2(value):
    high = value.astype(BF16)
    return high, (value - high.astype(F32)).astype(BF16)


def split3(value):
    high = value.astype(BF16)
    rest = value - high.astype(F32)
    mid = rest.astype(BF16)
    return high, mid, (rest - mid.astype(F32)).astype(BF16)


def kernel(
    matrix_ref, signs_ref, samples_ref, sketch_ref, factors_ref,
    X, SIB, P1, R1, R2, R3, R4, T3, R5, Y8, IDX, SGN, SMP, ML, OW, EB, FT, ET, POS, WF, WALL, G, RG1, RG2, GF, DUM,
    load_sem, in_sem, y_send, y_recv, p_send, p_recv, sib_send, sib_recv,
    e_send, e_recv, x_send, x_recv, s1, r1, s2, r2, s3, r3, s4, r4, s5, r5,
    w_send, w_recv, g1_send, g1_recv, g2_send, g2_recv, g3_send, g3_recv,
    o_send, o_recv, f_send, f_recv,
):
    me = lax.axis_index("rows")
    core = me % 2
    y_pos = (me // 2) % 4
    x_pos = (me // 8) % 4
    z_pos = me // 32
    sibling = me + 1 - 2 * core

    def along(stride, hop):
        pos = (me // stride) % 4
        return me + ((pos + hop) % 4 - pos) * stride

    def send(src, dst, send_sem, recv_sem, device):
        copy = pltpu.make_async_remote_copy(
            src_ref=src, dst_ref=dst, send_sem=send_sem, recv_sem=recv_sem,
            device_id=(device,), device_id_type=MESH,
        )
        copy.start()

    def wait(ref, sem):
        pltpu.make_async_copy(ref, ref, sem).wait()

    def load(chunk):
        return pltpu.make_async_copy(matrix_ref.at[chunk], X.at[chunk], load_sem.at[chunk])

    fetch_samples = pltpu.make_async_copy(samples_ref, SMP, in_sem.at[0])
    fetch_samples.start()
    fetch_signs = pltpu.make_async_copy(signs_ref, SGN, in_sem.at[1])
    fetch_signs.start()
    for chunk in range(16):
        load(chunk).start()

    group = [(dy, dc) for dy in range(4) for dc in range(2) if (dy, dc) != (0, 0)]
    plane = [(dz, dx) for dz in range(4) for dx in range(4) if (dz, dx) != (0, 0)]

    def mate(dy, dc):
        return along(2, dy) + dc * (1 - 2 * core)

    def peer(dz, dx):
        return ((z_pos + dz) % 4) * 32 + ((x_pos + dx) % 4) * 8 + me % 8

    barrier = pltpu.get_barrier_semaphore()
    for dy, dc in group:
        pl.semaphore_signal(barrier, inc=1, device_id=(mate(dy, dc),), device_id_type=MESH)
    for dz, dx in plane:
        pl.semaphore_signal(barrier, inc=1, device_id=(peer(dz, dx),), device_id_type=MESH)

    had = (1 - 2 * odd(iota((128, 128), 0) & iota((128, 128), 1))).astype(F32)
    fetch_samples.wait()

    samples = SMP[...]
    part = (samples >> 7) & 127
    intervals = jnp.concatenate([part[0:1], part[1:2]], axis=1)
    values = jnp.concatenate([samples[0:1], samples[1:2]], axis=1)
    onehot = iota((128, 256), 0) == intervals
    onehot_f = jnp.where(onehot, 1.0, 0.0)
    before = jnp.where(iota((256, 256), 0) < iota((256, 256), 1), 1.0, 0.0).astype(BF16)
    count = jnp.dot(onehot_f.astype(BF16), before, preferred_element_type=F32)
    rank = jnp.sum(count * onehot_f, axis=0, keepdims=True).astype(I32)
    place = (
        (intervals >> 6) * 128 + (intervals & 7) * 16 + ((intervals >> 3) & 7) * 2 + rank
    )
    POS[...] = place
    slot = rank * 128 + intervals
    chosen = jnp.where(iota((256, 256), 0) == slot, 1.0, 0.0).astype(BF16)
    row8 = iota((8, 256), 0)
    fields = jnp.where(row8 == 0, values & 127, jnp.where(row8 == 1, values >> 14, 0))
    sorted_fields = lax.dot_general(
        fields.astype(F32).astype(BF16), chosen, (((1,), (1,)), ((), ())), preferred_element_type=F32
    ).astype(I32)
    sorted_rows = (
        sorted_fields[1:2] * 16384 + (iota((1, 256), 1) & 127) * 128 + sorted_fields[0:1]
    )
    mine8 = 2 * y_pos + core
    Y8[mine8, 0:1, :] = sorted_rows[:, :128]
    Y8[mine8, 1:2, :] = sorted_rows[:, 128:]
    def front(chunk, carry):
        load(chunk).wait()
        for al in range(8):
            high, low = split2(X[chunk, al])
            sign = SGN[pl.ds(chunk * 8 + al, 1), :].astype(F32)
            signed = (had * sign).astype(BF16)
            X[chunk, al] = jnp.dot(
                jnp.concatenate([signed, signed], axis=1),
                jnp.concatenate([high, low], axis=0),
                preferred_element_type=F32,
            )
        for tile in range(16):
            rows = slice(8 * tile, 8 * tile + 8)
            v = [X[chunk, al, rows, :] for al in range(8)]
            for span in (1, 2, 4):
                v = butterfly(v, span)
            for al in range(8):
                X[chunk, al, rows, :] = v[al]
        return carry

    def butterfly(v, span):
        out = list(v)
        for n in range(len(v)):
            if n & span == 0:
                out[n] = v[n] + v[n + span]
                out[n + span] = v[n] - v[n + span]
        return out

    fetch_signs.wait()
    lax.fori_loop(0, 4, front, 0, unroll=2)
    pl.semaphore_wait(barrier, 22)
    for n, (dy, dc) in enumerate(group):
        send(Y8.at[mine8], Y8.at[mine8], y_send.at[n], y_recv.at[n], mate(dy, dc))
    lax.fori_loop(4, 14, front, 0, unroll=2)
    for n in range(7):
        wait(Y8.at[0], y_recv.at[n])
    for q in range(8):
        for j in range(2):
            IDX[z_pos, x_pos, j, q : q + 1, :] = Y8[q, j : j + 1, :]
    for dz, dx in plane:
        send(IDX.at[z_pos, x_pos], IDX.at[z_pos, x_pos], p_send, p_recv, peer(dz, dx))
    lax.fori_loop(14, 16, front, 0, unroll=2)

    def second(step):
        def tile_step(tile, carry):
            rows = pl.ds(pl.multiple_of(tile * 8, 8), 8)
            v = [X[ah, step, rows, :] for ah in range(16)]
            for span in (1, 2, 4, 8):
                v = butterfly(v, span)
            for ah in range(16):
                X[ah, step, rows, :] = v[ah]
            return carry

        lax.fori_loop(0, 16, tile_step, 0, unroll=2)
        send(
            X.at[pl.ds((1 - core) * 8, 8), step], SIB.at[step], sib_send.at[step], sib_recv.at[step], sibling
        )

    def axis_of(order, stage):
        k = (order + stage) % 3
        stride = 32 - 33 * k + 9 * k * k
        return stride, (me // stride) % 4

    def block_of(s, q, sib):
        return SIB.at[q // 2, 2 * s + q % 2] if sib else X.at[core * 8 + 2 * s + q % 2, q // 2]

    def early_send(sib):
        for s in range(3):
            stride, a = axis_of(s, 0)
            for hop in (1, 2, 3):
                send(
                    block_of(s, (a + hop) % 4, sib), EB.at[s, a, sib], e_send.at[s], e_recv.at[s],
                    along(stride, hop),
                )

    second(0)
    second(1)
    early_send(0)
    second(2)
    second(3)
    wait(SIB.at[0], sib_recv.at[0])
    wait(SIB.at[1], sib_recv.at[1])
    early_send(1)
    for s in range(3):
        _, a = axis_of(s, 0)
        for sib in (0, 1):
            EB[s, a, sib] = block_of(s, a, sib)[...]
    for step in range(4, TICKS):
        second(step)

    wait(DUM, p_recv)
    from_t = iota((128, 128), 0)
    to_t = iota((128, 128), 1)
    hi_t, mid_t, lo_t, core_t = to_t // 32, (to_t // 8) % 4, (to_t // 2) % 4, to_t % 2
    natural = [
        hi_t * 32 + mid_t * 8 + lo_t * 2 + core_t,
        hi_t * 8 + mid_t * 2 + lo_t * 32 + core_t,
        hi_t * 2 + mid_t * 32 + lo_t * 8 + core_t,
    ]
    for order in range(3):
        perm = jnp.where(from_t == natural[order], 1.0, 0.0).astype(BF16)
        for j in range(2):
            rows = IDX[:, :, j].reshape(128, 128)
            low = (rows & 127).astype(F32).astype(BF16)
            block = (rows >> 14).astype(F32).astype(BF16)
            ML[order, j] = dot_tt(low, perm).astype(I32)
            OW[order, j] = dot_tt(block, perm).astype(I32)

    sub = iota((128, 128), 0)

    def order_of(s, tick):
        return s if s < 3 else tick % 3

    def picked(order, p, device, own, sib):
        picks = []
        for j in range(2):
            hit = sub == ML[order, j, pl.ds(p, 1), :]
            owner = OW[order, j, pl.ds(p, 1), :]
            for bits in (owner & device, owner & (device + 1 - 2 * core)):
                picks.append(jnp.where(hit, (1 - 2 * odd(bits)).astype(F32), 0.0).astype(BF16))
        pick = jnp.concatenate(
            [jnp.concatenate(picks[:2], axis=0), jnp.concatenate(picks[2:], axis=0)], axis=1
        )
        own_hi, own_lo = split2(own)
        sib_hi, sib_lo = split2(sib)
        terms = jnp.concatenate(
            [jnp.concatenate([own_hi, sib_hi], axis=0), jnp.concatenate([own_lo, sib_lo], axis=0)], axis=1
        )
        got = dot_tt(pick, terms)
        return got[:, :128] + got[:, 128:]

    def produce(tick, first):
        def one(n, carry):
            s = n // 2
            order = s + (s // 3) * (tick % 3 - 3)
            p = (core * 8 + n) * 8 + tick
            got = picked(order, p, me, X[core * 8 + n, tick], SIB[tick, n])
            P1[tick, s, n % 2] = got.reshape(2, 4, 4, 8, 128)
            return carry

        lax.fori_loop(first, 8, one, 0, unroll=8 - first)

    def produce_early(s, carry):
        stride, a = axis_of(s, 0)
        p = (core * 8 + 2 * s + a % 2) * 8 + a // 2
        wait(EB.at[0, pl.ds(0, 3)], e_recv.at[s])
        got = sum(picked(s, p, me + (q - a) * stride, EB[s, q, 0], EB[s, q, 1]) for q in range(4))
        got = got.reshape(2, 4, 4, 8, 128)
        for q in range(4):
            for j in range(2):
                P1[q // 2, s, q % 2, j, a] = got[j, q]
        return carry

    def spread(tick, s, slabs, far, sems, stride, pos):
        over = (pos + 2) % 4
        for half, hop in ((0, 1), (1, 3)):
            send(slabs(over).at[:, half], far.at[tick, s, :, half], *sems, along(stride, hop))

    def relay(tick, s, slabs, near, far, sems, stride, pos):
        near_send, near_recv = sems
        for slot, hop in ((0, 1), (1, 3)):
            slab = slabs((pos + hop) % 4)
            slab[:, slot] += far[tick, s, :, slot]
            send(slab, near.at[tick, s, slot], near_send, near_recv, along(stride, hop))

    def slabs_of(tick, s):
        return lambda q: P1.at[tick, s, :, :, q]

    def parts_of(tick, s, a):
        return lambda q: P1.at[tick, s, :, :, a, q]

    def wait_streams(ref, sem, tick, streams):
        wait(ref.at[tick] if len(streams) == STREAMS else ref.at[tick, 3], sem.at[tick])

    def first_send(tick, streams):
        for s in streams:
            spread(tick, s, slabs_of(tick, s), R1, (s1.at[tick], r1.at[tick]), *axis_of(order_of(s, tick), 0))

    def first_pass(tick, streams):
        wait_streams(R1, r1, tick, streams)
        for s in streams:
            sems = (s2.at[tick], r2.at[tick])
            relay(tick, s, slabs_of(tick, s), R2, R1, sems, *axis_of(order_of(s, tick), 0))

    def second_send(tick, streams):
        wait_streams(R2, r2, tick, streams)
        for s in range(STREAMS):
            _, a = axis_of(order_of(s, tick), 0)
            if s in streams:
                P1[tick, s, :, :, a] += R2[tick, s, 0] + R2[tick, s, 1]
            spread(tick, s, parts_of(tick, s, a), R3, (s3.at[tick], r3.at[tick]), *axis_of(order_of(s, tick), 1))

    def second_pass(tick, streams):
        wait(R3.at[tick], r3.at[tick])
        for s in range(STREAMS):
            _, a = axis_of(order_of(s, tick), 0)
            sems = (s4.at[tick], r4.at[tick])
            relay(tick, s, parts_of(tick, s, a), R4, R3, sems, *axis_of(order_of(s, tick), 1))

    def third_send(tick, streams):
        wait(R4.at[tick], r4.at[tick])
        for s in range(STREAMS):
            _, a = axis_of(order_of(s, tick), 0)
            _, b = axis_of(order_of(s, tick), 1)
            total = P1[tick, s, :, :, a, b] + R4[tick, s, 0] + R4[tick, s, 1]
            for g in range(2):
                for j in range(2):
                    for q in range(4):
                        for ct in range(2):
                            row = ct * 4 + g * 2 + j
                            T3[tick, s, q, row : row + 1, :] = total[g, j, 2 * q + ct : 2 * q + ct + 1, :]
            stride, d = axis_of(order_of(s, tick), 2)
            for hop in (1, 2, 3):
                send(
                    T3.at[tick, s, (d + hop) % 4], R5.at[tick, s, hop - 1], s5.at[tick], r5.at[tick],
                    along(stride, hop),
                )

    scale = 1.0 / math.sqrt(ROWS)

    def last(tick, streams):
        wait(R5.at[tick], r5.at[tick])
        done = []
        for s in range(STREAMS):
            _, d = axis_of(order_of(s, tick), 2)
            done.append((T3[tick, s, d] + R5[tick, s, 0] + R5[tick, s, 1] + R5[tick, s, 2]) * scale)
            if s not in streams:
                FT[tick, s] = done[s]
        if len(streams) < STREAMS:
            for ct in range(2):
                WF[ct, pl.ds(pl.multiple_of(tick * 16 + 8, 8), 8), :] = jnp.concatenate(
                    [done[3][4 * ct : 4 * ct + 4]] * 2, axis=0
                )
            return
        for ct in range(2):
            for pair in range(2):
                rows = pl.ds(pl.multiple_of(tick * 16 + pair * 8, 8), 8)
                WF[ct, rows, :] = jnp.concatenate(
                    [done[2 * pair][4 * ct : 4 * ct + 4], done[2 * pair + 1][4 * ct : 4 * ct + 4]], axis=0
                )

    def make(tick, streams):
        if len(streams) == STREAMS:
            wait(SIB.at[tick], sib_recv.at[tick])
        produce(tick, 2 * streams[0])
        first_send(tick, streams)

    everything, late = (0, 1, 2, 3), (3,)

    def each(work, start, stop, streams):
        def step(tick, carry):
            work(tick, streams)
            return carry

        lax.fori_loop(start, stop, step, 0)

    for work in (make, first_pass, second_send, second_pass, third_send, last):
        each(work, 0, EARLY, late)
        if work is last:
            for s in range(3):
                stride, a = axis_of(s, 0)
                for hop in (1, 2, 3):
                    send(FT.at[((a + hop) % 4) // 2, s], ET.at[s, a], x_send.at[s], x_recv.at[s], along(stride, hop))
                ET[s, a] = FT[a // 2, s]
        each(work, EARLY, TICKS, everything)
        if work is first_pass:
            lax.fori_loop(0, 3, produce_early, 0)

    for s in range(3):
        wait(ET.at[0, pl.ds(0, 3)], x_recv.at[s])
    for tick in range(EARLY):
        for ct in range(2):
            rows = []
            for s in range(3):
                _, a = axis_of(s, 0)
                for g in range(2):
                    tile = ET[s, 2 * tick + g]
                    pair = [tile[4 * ct + 2 * n : 4 * ct + 2 * n + 2] for n in range(2)]
                    rows.append(jnp.where(a % 2 == 0, pair[0], pair[1]))
            rows.append(WF[ct, 16 * tick + 12 : 16 * tick + 16, :])
            WF[ct, 16 * tick : 16 * tick + 16, :] = jnp.concatenate(rows, axis=0)

    send(WF.at[1 - core], WALL.at[core], w_send, w_recv, sibling)
    high, mid, low = split3(WF[...].reshape(256, 128))
    square = dot_tt(high, jnp.concatenate([high, mid], axis=1))
    rest = dot_tt(mid, jnp.concatenate([mid, low], axis=1))
    outer = dot_tt(high, low)
    cross = square[:, 128:] + outer
    gram = square[:, :128] + rest[:, :128] + (cross + cross.T)
    G[...] = (gram * (1.0 / SAMP_OWN)).reshape(2, 64, 128)
    send(G.at[1 - core], RG1, g1_send, g1_recv, sibling)
    wait(RG1, g1_recv)
    G[core] += RG1[...]
    for hop in (1, 2, 3):
        send(G.at[core], RG2.at[hop - 1], g2_send.at[hop - 1], g2_recv.at[hop - 1], along(2, hop))

    WALL[core] = WF[core]
    wait(WALL.at[0], w_recv)
    back = jnp.where(iota((256, 256), 0) == POS[...], 1.0, 0.0).astype(BF16)
    sketch_ref[...] = sum(dot_tt(back, term) for term in split3(WALL[...].reshape(256, 128)))

    for hop in (1, 2, 3):
        wait(RG2.at[0], g2_recv.at[hop - 1])
    terms = [G[core], RG2[0], RG2[1], RG2[2]]
    GF[core] = (terms[0] + terms[2]) + (terms[1] + terms[3])
    send(GF.at[core], GF.at[core], g3_send, g3_recv, sibling)
    wait(GF.at[0], g3_recv)

    sub16 = iota((16, 128), 0)
    lane16 = iota((16, 128), 1)
    work = GF[...].reshape(128, 128)
    for r in range(8):
        panel = work[:16]
        columns = [jnp.broadcast_to(panel[:, 16 * r + k : 16 * r + k + 1], (16, 128)) for k in range(16)]
        scales = jnp.zeros((16, 128), F32)
        for j in range(16):
            inverse = lax.rsqrt(columns[j][j : j + 1])
            square = inverse * inverse
            below = jnp.where(sub16 > j, columns[j], 0.0)
            scales = jnp.where(sub16 == j, inverse, scales)
            for k in range(j + 1, 16):
                columns[k] = columns[k] - (below * columns[k][j : j + 1]) * square
            panel = panel - (below * panel[j : j + 1]) * square
        panel = jnp.where(lane16 >= 16 * r + sub16, panel * scales, 0.0)

        @pl.when(core == r % 2)
        def _():
            factors_ref[z_pos, x_pos, r] = panel
            block = factors_ref.at[z_pos, x_pos, r]
            for dz, dx in plane:
                send(block, block, o_send.at[r // 2], o_recv.at[r // 2], peer(dz, dx))

        if r < 7:
            h, m, l = (term.astype(F32) for term in split3(panel))
            lhs = jnp.concatenate([h, h, m, m, h, l], axis=0).astype(BF16)
            rhs = jnp.concatenate([h, m, h, m, l, h], axis=0).astype(BF16)
            work = work[16:] - dot_tt(lhs, rhs)[16 * r + 16 :]

    def share(n):
        slab = factors_ref.at[:, :, 2 * n + core]
        wait(DUM, o_recv.at[n])
        send(slab, slab, f_send.at[n], f_recv.at[n], sibling)

    for n in range(2):
        share(n)

    for n in range(7):
        wait(Y8.at[0], y_send.at[n])
    wait(DUM, p_send)
    for n in range(3):
        wait(RG2.at[0], g2_send.at[n])
    wait(GF.at[0], g3_send)
    wait(RG1, g1_send)
    wait(WALL.at[0], w_send)

    for s in range(3):
        wait(EB.at[0, pl.ds(0, 3)], e_send.at[s])
        wait(ET.at[0, pl.ds(0, 3)], x_send.at[s])

    def sent(tick, streams):
        wait(SIB.at[tick], sib_send.at[tick])
        wait_streams(R1, s1, tick, streams)
        wait_streams(R2, s2, tick, streams)
        wait(R3.at[tick], s3.at[tick])
        wait(R4.at[tick], s4.at[tick])
        wait(R5.at[tick], s5.at[tick])

    each(sent, 0, EARLY, late)
    each(sent, EARLY, TICKS, everything)

    for n in range(2, 4):
        share(n)
    for n in range(4):
        wait(factors_ref.at[:, :, 0], f_recv.at[n])
    for n in range(4):
        wait(DUM, o_send.at[n])
        wait(factors_ref.at[:, :, 0], f_send.at[n])


def body(matrix, signs, samples):
    dma = pltpu.SemaphoreType.DMA
    vmem = pltpu.VMEM
    t, s = TICKS, STREAMS
    sketch, factors = pl.pallas_call(
        kernel,
        out_shape=(
            jax.ShapeDtypeStruct((256, 128), F32),
            jax.ShapeDtypeStruct((4, 4, 8, 16, 128), F32),
        ),
        in_specs=[pl.BlockSpec(memory_space=pltpu.HBM)] * 3,
        out_specs=(pl.BlockSpec(memory_space=pltpu.VMEM), pl.BlockSpec(memory_space=pltpu.VMEM)),
        scratch_shapes=[
            vmem((16, 8, 128, 128), F32),
            vmem((8, 8, 128, 128), F32),
            vmem((t, s, 2, 2, 4, 4, 8, 128), F32),
            vmem((t, s, 2, 2, 4, 8, 128), F32),
            vmem((t, s, 2, 2, 2, 4, 8, 128), F32),
            vmem((t, s, 2, 2, 8, 128), F32),
            vmem((t, s, 2, 2, 2, 8, 128), F32),
            vmem((t, s, 4, 8, 128), F32),
            vmem((t, s, 3, 8, 128), F32),
            vmem((8, 8, 128), I32),
            vmem((4, 4, 2, 8, 128), I32),
            vmem((128, 128), I32),
            vmem((2, 128), I32),
            vmem((3, 2, 128, 128), I32),
            vmem((3, 2, 128, 128), I32),
            vmem((3, 4, 2, 128, 128), F32),
            vmem((2, 3, 8, 128), F32),
            vmem((3, 4, 8, 128), F32),
            vmem((1, 256), I32),
            vmem((2, 128, 128), F32),
            vmem((2, 128, 128), F32),
            vmem((2, 64, 128), F32),
            vmem((64, 128), F32),
            vmem((3, 64, 128), F32),
            vmem((2, 64, 128), F32),
            vmem((15, 16, 128), F32),
            dma((16,)), dma((2,)), dma((7,)), dma((7,)), dma(()), dma(()),
            dma((t,)), dma((t,)),
            dma((3,)), dma((3,)), dma((3,)), dma((3,)),
            dma((t,)), dma((t,)), dma((t,)), dma((t,)), dma((t,)), dma((t,)), dma((t,)), dma((t,)),
            dma((t,)), dma((t,)),
            dma(()), dma(()), dma(()), dma(()), dma((3,)), dma((3,)), dma(()), dma(()),
            dma((4,)), dma((4,)), dma((4,)), dma((4,)),
        ],
        compiler_params=pltpu.CompilerParams(
            collective_id=0, has_side_effects=True, vmem_limit_bytes=48 * 1024 * 1024
        ),
    )(matrix.reshape(16, 8, 128, 128), signs.reshape(128, 128), samples.reshape(2, 128))
    return sketch, factors.reshape(16, 128, 128)


def solution(mesh):
    return jax.shard_map(
        body,
        mesh=mesh,
        in_specs=(P("rows", None), P("rows"), P("rows")),
        out_specs=(P("rows", None), P()),
        check_vma=False,
    )
```

```python
import functools
import math

import jax
import jax.numpy as jnp
from jax import lax
from jax.experimental import pallas as pl
from jax.experimental.pallas import tpu as pltpu
from jax.sharding import PartitionSpec as P

MESH = pl.DeviceIdType.MESH
F32 = jnp.float32
BF16 = jnp.bfloat16
I32 = jnp.int32

TICKS = 8
EARLY = 2
STREAMS = 4
ROWS = 2097152
SAMP_OWN = 2048


def dot_tt(lhs, rhs, precision=None):
    return lax.dot_general(
        lhs, rhs, (((0,), (0,)), ((), ())), precision=precision, preferred_element_type=F32
    )


def iota(shape, dim):
    return lax.broadcasted_iota(I32, shape, dim)


def odd(bits):
    bits = bits ^ (bits >> 4)
    bits = bits ^ (bits >> 2)
    bits = bits ^ (bits >> 1)
    return bits & 1


def split2(value):
    high = value.astype(BF16)
    return high, (value - high.astype(F32)).astype(BF16)


def split3(value):
    high = value.astype(BF16)
    rest = value - high.astype(F32)
    mid = rest.astype(BF16)
    return high, mid, (rest - mid.astype(F32)).astype(BF16)


def kernel(
    matrix_ref, small_ref, sketch_ref, factors_ref,
    X, SIB, P1, R1, R2, R3, R4, T3, R5, Y8, IDX, ML, OW, EB, FT, ET, POS, WF, WALL, G, RG1, RG2, GF, DUM,
    load_sem, y_send, y_recv, p_send, p_recv, sib_send, sib_recv,
    e_send, e_recv, x_send, x_recv, s1, r1, s2, r2, s3, r3, s4, r4, s5, r5,
    w_send, w_recv, g1_send, g1_recv, g2_send, g2_recv, g3_send, g3_recv,
    o_send, o_recv, f_send, f_recv,
):
    me = lax.axis_index("rows")
    core = me % 2
    y_pos = (me // 2) % 4
    x_pos = (me // 8) % 4
    z_pos = me // 32
    sibling = me + 1 - 2 * core

    def along(stride, hop):
        pos = (me // stride) % 4
        return me + ((pos + hop) % 4 - pos) * stride

    def send(src, dst, send_sem, recv_sem, device):
        copy = pltpu.make_async_remote_copy(
            src_ref=src, dst_ref=dst, send_sem=send_sem, recv_sem=recv_sem,
            device_id=(device,), device_id_type=MESH,
        )
        copy.start()

    def wait(ref, sem):
        pltpu.make_async_copy(ref, ref, sem).wait()

    def load(chunk):
        return pltpu.make_async_copy(matrix_ref.at[chunk], X.at[chunk], load_sem.at[chunk])

    for chunk in range(16):
        load(chunk).start()

    group = [(dy, dc) for dy in range(4) for dc in range(2) if (dy, dc) != (0, 0)]
    plane = [(dz, dx) for dz in range(4) for dx in range(4) if (dz, dx) != (0, 0)]

    def mate(dy, dc):
        return along(2, dy) + dc * (1 - 2 * core)

    def peer(dz, dx):
        return ((z_pos + dz) % 4) * 32 + ((x_pos + dx) % 4) * 8 + me % 8

    barrier = pltpu.get_barrier_semaphore()
    for dy, dc in group:
        pl.semaphore_signal(barrier, inc=1, device_id=(mate(dy, dc),), device_id_type=MESH)
    for dz, dx in plane:
        pl.semaphore_signal(barrier, inc=1, device_id=(peer(dz, dx),), device_id_type=MESH)

    had = (1 - 2 * odd(iota((128, 128), 0) & iota((128, 128), 1))).astype(F32)

    samples = small_ref[128:130, :]
    part = (samples >> 7) & 127
    intervals = jnp.concatenate([part[0:1], part[1:2]], axis=1)
    values = jnp.concatenate([samples[0:1], samples[1:2]], axis=1)
    onehot = iota((128, 256), 0) == intervals
    onehot_f = jnp.where(onehot, 1.0, 0.0)
    before = jnp.where(iota((256, 256), 0) < iota((256, 256), 1), 1.0, 0.0).astype(BF16)
    count = jnp.dot(onehot_f.astype(BF16), before, preferred_element_type=F32)
    rank = jnp.sum(count * onehot_f, axis=0, keepdims=True).astype(I32)
    place = (
        (intervals >> 6) * 128 + (intervals & 7) * 16 + ((intervals >> 3) & 7) * 2 + rank
    )
    POS[...] = place
    slot = rank * 128 + intervals
    chosen = jnp.where(iota((256, 256), 0) == slot, 1.0, 0.0).astype(BF16)
    row8 = iota((8, 256), 0)
    fields = jnp.where(row8 == 0, values & 127, jnp.where(row8 == 1, values >> 14, 0))
    sorted_fields = lax.dot_general(
        fields.astype(F32).astype(BF16), chosen, (((1,), (1,)), ((), ())), preferred_element_type=F32
    ).astype(I32)
    sorted_rows = (
        sorted_fields[1:2] * 16384 + (iota((1, 256), 1) & 127) * 128 + sorted_fields[0:1]
    )
    mine8 = 2 * y_pos + core
    Y8[mine8, 0:1, :] = sorted_rows[:, :128]
    Y8[mine8, 1:2, :] = sorted_rows[:, 128:]
    def front(chunk, carry):
        load(chunk).wait()
        for al in range(8):
            high, low = split2(X[chunk, al])
            sign = small_ref[pl.ds(chunk * 8 + al, 1), :].astype(F32)
            signed = (had * sign).astype(BF16)
            X[chunk, al] = jnp.dot(
                jnp.concatenate([signed, signed], axis=1),
                jnp.concatenate([high, low], axis=0),
                preferred_element_type=F32,
            )
        for tile in range(16):
            rows = slice(8 * tile, 8 * tile + 8)
            v = [X[chunk, al, rows, :] for al in range(8)]
            for span in (1, 2, 4):
                v = butterfly(v, span)
            for al in range(8):
                X[chunk, al, rows, :] = v[al]
        return carry

    def butterfly(v, span):
        out = list(v)
        for n in range(len(v)):
            if n & span == 0:
                out[n] = v[n] + v[n + span]
                out[n + span] = v[n] - v[n + span]
        return out

    lax.fori_loop(0, 4, front, 0, unroll=2)
    pl.semaphore_wait(barrier, 22)
    for n, (dy, dc) in enumerate(group):
        send(Y8.at[mine8], Y8.at[mine8], y_send.at[n], y_recv.at[n], mate(dy, dc))
    lax.fori_loop(4, 14, front, 0, unroll=2)
    for n in range(7):
        wait(Y8.at[0], y_recv.at[n])
    for q in range(8):
        for j in range(2):
            IDX[z_pos, x_pos, j, q : q + 1, :] = Y8[q, j : j + 1, :]
    for dz, dx in plane:
        send(IDX.at[z_pos, x_pos], IDX.at[z_pos, x_pos], p_send, p_recv, peer(dz, dx))
    lax.fori_loop(14, 16, front, 0, unroll=2)

    def second(step):
        def tile_step(tile, carry):
            rows = pl.ds(pl.multiple_of(tile * 8, 8), 8)
            v = [X[ah, step, rows, :] for ah in range(16)]
            for span in (1, 2, 4, 8):
                v = butterfly(v, span)
            for ah in range(16):
                X[ah, step, rows, :] = v[ah]
            return carry

        lax.fori_loop(0, 16, tile_step, 0, unroll=2)
        send(
            X.at[pl.ds((1 - core) * 8, 8), step], SIB.at[step], sib_send.at[step], sib_recv.at[step], sibling
        )

    def axis_of(order, stage):
        k = (order + stage) % 3
        stride = 32 - 33 * k + 9 * k * k
        return stride, (me // stride) % 4

    def block_of(s, q, sib):
        return SIB.at[q // 2, 2 * s + q % 2] if sib else X.at[core * 8 + 2 * s + q % 2, q // 2]

    def early_send(sib):
        for s in range(3):
            stride, a = axis_of(s, 0)
            for hop in (1, 2, 3):
                send(
                    block_of(s, (a + hop) % 4, sib), EB.at[s, a, sib], e_send.at[s], e_recv.at[s],
                    along(stride, hop),
                )

    second(0)
    second(1)
    early_send(0)
    second(2)
    second(3)
    wait(SIB.at[0], sib_recv.at[0])
    wait(SIB.at[1], sib_recv.at[1])
    early_send(1)
    for s in range(3):
        _, a = axis_of(s, 0)
        for sib in (0, 1):
            EB[s, a, sib] = block_of(s, a, sib)[...]
    for step in range(4, TICKS):
        second(step)

    wait(DUM, p_recv)
    from_t = iota((128, 128), 0)
    to_t = iota((128, 128), 1)
    hi_t, mid_t, lo_t, core_t = to_t // 32, (to_t // 8) % 4, (to_t // 2) % 4, to_t % 2
    natural = [
        hi_t * 32 + mid_t * 8 + lo_t * 2 + core_t,
        hi_t * 8 + mid_t * 2 + lo_t * 32 + core_t,
        hi_t * 2 + mid_t * 32 + lo_t * 8 + core_t,
    ]
    for order in range(3):
        perm = jnp.where(from_t == natural[order], 1.0, 0.0).astype(BF16)
        for j in range(2):
            rows = IDX[:, :, j].reshape(128, 128)
            low = (rows & 127).astype(F32).astype(BF16)
            block = (rows >> 14).astype(F32).astype(BF16)
            ML[order, j] = dot_tt(low, perm).astype(I32)
            OW[order, j] = dot_tt(block, perm).astype(I32)

    sub = iota((128, 128), 0)

    def order_of(s, tick):
        return s if s < 3 else tick % 3

    def picked(order, p, device, own, sib):
        picks = []
        for j in range(2):
            hit = sub == ML[order, j, pl.ds(p, 1), :]
            owner = OW[order, j, pl.ds(p, 1), :]
            for bits in (owner & device, owner & (device + 1 - 2 * core)):
                picks.append(jnp.where(hit, (1 - 2 * odd(bits)).astype(F32), 0.0).astype(BF16))
        pick = jnp.concatenate(
            [jnp.concatenate(picks[:2], axis=0), jnp.concatenate(picks[2:], axis=0)], axis=1
        )
        own_hi, own_lo = split2(own)
        sib_hi, sib_lo = split2(sib)
        terms = jnp.concatenate(
            [jnp.concatenate([own_hi, sib_hi], axis=0), jnp.concatenate([own_lo, sib_lo], axis=0)], axis=1
        )
        got = dot_tt(pick, terms)
        return got[:, :128] + got[:, 128:]

    def produce(tick, first):
        def one(n, carry):
            s = n // 2
            order = s + (s // 3) * (tick % 3 - 3)
            p = (core * 8 + n) * 8 + tick
            got = picked(order, p, me, X[core * 8 + n, tick], SIB[tick, n])
            P1[tick, s, n % 2] = got.reshape(2, 4, 4, 8, 128)
            return carry

        lax.fori_loop(first, 8, one, 0, unroll=8 - first)

    def produce_early(s, carry):
        stride, a = axis_of(s, 0)
        p = (core * 8 + 2 * s + a % 2) * 8 + a // 2
        wait(EB.at[0, pl.ds(0, 3)], e_recv.at[s])
        got = sum(picked(s, p, me + (q - a) * stride, EB[s, q, 0], EB[s, q, 1]) for q in range(4))
        got = got.reshape(2, 4, 4, 8, 128)
        for q in range(4):
            for j in range(2):
                P1[q // 2, s, q % 2, j, a] = got[j, q]
        return carry

    def spread(tick, s, slabs, far, sems, stride, pos):
        over = (pos + 2) % 4
        for half, hop in ((0, 1), (1, 3)):
            send(slabs(over).at[:, half], far.at[tick, s, :, half], *sems, along(stride, hop))

    def relay(tick, s, slabs, near, far, sems, stride, pos):
        near_send, near_recv = sems
        for slot, hop in ((0, 1), (1, 3)):
            slab = slabs((pos + hop) % 4)
            slab[:, slot] += far[tick, s, :, slot]
            send(slab, near.at[tick, s, slot], near_send, near_recv, along(stride, hop))

    def slabs_of(tick, s):
        return lambda q: P1.at[tick, s, :, :, q]

    def parts_of(tick, s, a):
        return lambda q: P1.at[tick, s, :, :, a, q]

    def wait_streams(ref, sem, tick, streams):
        wait(ref.at[tick] if len(streams) == STREAMS else ref.at[tick, 3], sem.at[tick])

    def first_send(tick, streams):
        for s in streams:
            spread(tick, s, slabs_of(tick, s), R1, (s1.at[tick], r1.at[tick]), *axis_of(order_of(s, tick), 0))

    def first_pass(tick, streams):
        wait_streams(R1, r1, tick, streams)
        for s in streams:
            sems = (s2.at[tick], r2.at[tick])
            relay(tick, s, slabs_of(tick, s), R2, R1, sems, *axis_of(order_of(s, tick), 0))

    def second_send(tick, streams):
        wait_streams(R2, r2, tick, streams)
        for s in range(STREAMS):
            _, a = axis_of(order_of(s, tick), 0)
            if s in streams:
                P1[tick, s, :, :, a] += R2[tick, s, 0] + R2[tick, s, 1]
            spread(tick, s, parts_of(tick, s, a), R3, (s3.at[tick], r3.at[tick]), *axis_of(order_of(s, tick), 1))

    def second_pass(tick, streams):
        wait(R3.at[tick], r3.at[tick])
        for s in range(STREAMS):
            _, a = axis_of(order_of(s, tick), 0)
            sems = (s4.at[tick], r4.at[tick])
            relay(tick, s, parts_of(tick, s, a), R4, R3, sems, *axis_of(order_of(s, tick), 1))

    def third_send(tick, streams):
        wait(R4.at[tick], r4.at[tick])
        for s in range(STREAMS):
            _, a = axis_of(order_of(s, tick), 0)
            _, b = axis_of(order_of(s, tick), 1)
            total = P1[tick, s, :, :, a, b] + R4[tick, s, 0] + R4[tick, s, 1]
            for g in range(2):
                for j in range(2):
                    for q in range(4):
                        for ct in range(2):
                            row = ct * 4 + g * 2 + j
                            T3[tick, s, q, row : row + 1, :] = total[g, j, 2 * q + ct : 2 * q + ct + 1, :]
            stride, d = axis_of(order_of(s, tick), 2)
            for hop in (1, 2, 3):
                send(
                    T3.at[tick, s, (d + hop) % 4], R5.at[tick, s, hop - 1], s5.at[tick], r5.at[tick],
                    along(stride, hop),
                )

    scale = 1.0 / math.sqrt(ROWS)

    def last(tick, streams):
        wait(R5.at[tick], r5.at[tick])
        done = []
        for s in range(STREAMS):
            _, d = axis_of(order_of(s, tick), 2)
            done.append((T3[tick, s, d] + R5[tick, s, 0] + R5[tick, s, 1] + R5[tick, s, 2]) * scale)
            if s not in streams:
                FT[tick, s] = done[s]
        if len(streams) < STREAMS:
            for ct in range(2):
                WF[ct, pl.ds(pl.multiple_of(tick * 16 + 8, 8), 8), :] = jnp.concatenate(
                    [done[3][4 * ct : 4 * ct + 4]] * 2, axis=0
                )
            return
        for ct in range(2):
            for pair in range(2):
                rows = pl.ds(pl.multiple_of(tick * 16 + pair * 8, 8), 8)
                WF[ct, rows, :] = jnp.concatenate(
                    [done[2 * pair][4 * ct : 4 * ct + 4], done[2 * pair + 1][4 * ct : 4 * ct + 4]], axis=0
                )

    def make(tick, streams):
        if len(streams) == STREAMS:
            wait(SIB.at[tick], sib_recv.at[tick])
        produce(tick, 2 * streams[0])
        first_send(tick, streams)

    everything, late = (0, 1, 2, 3), (3,)

    def each(work, start, stop, streams):
        def step(tick, carry):
            work(tick, streams)
            return carry

        lax.fori_loop(start, stop, step, 0)

    for work in (make, first_pass, second_send, second_pass, third_send, last):
        each(work, 0, EARLY, late)
        if work is last:
            for s in range(3):
                stride, a = axis_of(s, 0)
                for hop in (1, 2, 3):
                    send(FT.at[((a + hop) % 4) // 2, s], ET.at[s, a], x_send.at[s], x_recv.at[s], along(stride, hop))
                ET[s, a] = FT[a // 2, s]
        each(work, EARLY, TICKS, everything)
        if work is first_pass:
            lax.fori_loop(0, 3, produce_early, 0)

    for s in range(3):
        wait(ET.at[0, pl.ds(0, 3)], x_recv.at[s])
    for tick in range(EARLY):
        for ct in range(2):
            rows = []
            for s in range(3):
                _, a = axis_of(s, 0)
                for g in range(2):
                    tile = ET[s, 2 * tick + g]
                    pair = [tile[4 * ct + 2 * n : 4 * ct + 2 * n + 2] for n in range(2)]
                    rows.append(jnp.where(a % 2 == 0, pair[0], pair[1]))
            rows.append(WF[ct, 16 * tick + 12 : 16 * tick + 16, :])
            WF[ct, 16 * tick : 16 * tick + 16, :] = jnp.concatenate(rows, axis=0)

    send(WF.at[1 - core], WALL.at[core], w_send, w_recv, sibling)
    high, mid, low = split3(WF[...].reshape(256, 128))
    square = dot_tt(high, jnp.concatenate([high, mid], axis=1))
    rest = dot_tt(mid, jnp.concatenate([mid, low], axis=1))
    outer = dot_tt(high, low)
    cross = square[:, 128:] + outer
    gram = square[:, :128] + rest[:, :128] + (cross + cross.T)
    G[...] = (gram * (1.0 / SAMP_OWN)).reshape(2, 64, 128)
    send(G.at[1 - core], RG1, g1_send, g1_recv, sibling)
    wait(RG1, g1_recv)
    G[core] += RG1[...]
    for hop in (1, 2, 3):
        send(G.at[core], RG2.at[hop - 1], g2_send.at[hop - 1], g2_recv.at[hop - 1], along(2, hop))

    WALL[core] = WF[core]
    wait(WALL.at[0], w_recv)
    back = jnp.where(iota((256, 256), 0) == POS[...], 1.0, 0.0).astype(BF16)
    sketch_ref[...] = sum(dot_tt(back, term) for term in split3(WALL[...].reshape(256, 128)))

    for hop in (1, 2, 3):
        wait(RG2.at[0], g2_recv.at[hop - 1])
    terms = [G[core], RG2[0], RG2[1], RG2[2]]
    GF[core] = (terms[0] + terms[2]) + (terms[1] + terms[3])
    send(GF.at[core], GF.at[core], g3_send, g3_recv, sibling)
    wait(GF.at[0], g3_recv)

    sub16 = iota((16, 128), 0)
    lane16 = iota((16, 128), 1)
    work = GF[...].reshape(128, 128)
    for r in range(8):
        panel = work[:16]
        columns = [jnp.broadcast_to(panel[:, 16 * r + k : 16 * r + k + 1], (16, 128)) for k in range(16)]
        scales = jnp.zeros((16, 128), F32)
        for j in range(16):
            inverse = lax.rsqrt(columns[j][j : j + 1])
            square = inverse * inverse
            below = jnp.where(sub16 > j, columns[j], 0.0)
            scales = jnp.where(sub16 == j, inverse, scales)
            for k in range(j + 1, 16):
                columns[k] = columns[k] - (below * columns[k][j : j + 1]) * square
            panel = panel - (below * panel[j : j + 1]) * square
        panel = jnp.where(lane16 >= 16 * r + sub16, panel * scales, 0.0)

        @pl.when(core == r % 2)
        def _():
            factors_ref[z_pos, x_pos, r] = panel
            block = factors_ref.at[z_pos, x_pos, r]
            for dz, dx in plane:
                send(block, block, o_send.at[r // 2], o_recv.at[r // 2], peer(dz, dx))

        if r < 7:
            h, m, l = (term.astype(F32) for term in split3(panel))
            lhs = jnp.concatenate([h, h, m, m, h, l], axis=0).astype(BF16)
            rhs = jnp.concatenate([h, m, h, m, l, h], axis=0).astype(BF16)
            work = work[16:] - dot_tt(lhs, rhs)[16 * r + 16 :]

    def share(n):
        slab = factors_ref.at[:, :, 2 * n + core]
        wait(DUM, o_recv.at[n])
        send(slab, slab, f_send.at[n], f_recv.at[n], sibling)

    for n in range(2):
        share(n)

    for n in range(7):
        wait(Y8.at[0], y_send.at[n])
    wait(DUM, p_send)
    for n in range(3):
        wait(RG2.at[0], g2_send.at[n])
    wait(GF.at[0], g3_send)
    wait(RG1, g1_send)
    wait(WALL.at[0], w_send)

    for s in range(3):
        wait(EB.at[0, pl.ds(0, 3)], e_send.at[s])
        wait(ET.at[0, pl.ds(0, 3)], x_send.at[s])

    def sent(tick, streams):
        wait(SIB.at[tick], sib_send.at[tick])
        wait_streams(R1, s1, tick, streams)
        wait_streams(R2, s2, tick, streams)
        wait(R3.at[tick], s3.at[tick])
        wait(R4.at[tick], s4.at[tick])
        wait(R5.at[tick], s5.at[tick])

    each(sent, 0, EARLY, late)
    each(sent, EARLY, TICKS, everything)

    for n in range(2, 4):
        share(n)
    for n in range(4):
        wait(factors_ref.at[:, :, 0], f_recv.at[n])
    for n in range(4):
        wait(DUM, o_send.at[n])
        wait(factors_ref.at[:, :, 0], f_send.at[n])


def body(matrix, signs, samples):
    dma = pltpu.SemaphoreType.DMA
    vmem = pltpu.VMEM
    t, s = TICKS, STREAMS
    small = jnp.concatenate([signs, samples]).reshape(130, 128)
    sketch, factors = pl.pallas_call(
        kernel,
        out_shape=(
            jax.ShapeDtypeStruct((256, 128), F32),
            jax.ShapeDtypeStruct((4, 4, 8, 16, 128), F32),
        ),
        in_specs=[pl.BlockSpec(memory_space=pltpu.HBM), pl.BlockSpec(memory_space=pltpu.VMEM)],
        out_specs=(pl.BlockSpec(memory_space=pltpu.VMEM), pl.BlockSpec(memory_space=pltpu.VMEM)),
        scratch_shapes=[
            vmem((16, 8, 128, 128), F32),
            vmem((8, 8, 128, 128), F32),
            vmem((t, s, 2, 2, 4, 4, 8, 128), F32),
            vmem((t, s, 2, 2, 4, 8, 128), F32),
            vmem((t, s, 2, 2, 2, 4, 8, 128), F32),
            vmem((t, s, 2, 2, 8, 128), F32),
            vmem((t, s, 2, 2, 2, 8, 128), F32),
            vmem((t, s, 4, 8, 128), F32),
            vmem((t, s, 3, 8, 128), F32),
            vmem((8, 8, 128), I32),
            vmem((4, 4, 2, 8, 128), I32),
            vmem((3, 2, 128, 128), I32),
            vmem((3, 2, 128, 128), I32),
            vmem((3, 4, 2, 128, 128), F32),
            vmem((2, 3, 8, 128), F32),
            vmem((3, 4, 8, 128), F32),
            vmem((1, 256), I32),
            vmem((2, 128, 128), F32),
            vmem((2, 128, 128), F32),
            vmem((2, 64, 128), F32),
            vmem((64, 128), F32),
            vmem((3, 64, 128), F32),
            vmem((2, 64, 128), F32),
            vmem((15, 16, 128), F32),
            dma((16,)), dma((7,)), dma((7,)), dma(()), dma(()),
            dma((t,)), dma((t,)),
            dma((3,)), dma((3,)), dma((3,)), dma((3,)),
            dma((t,)), dma((t,)), dma((t,)), dma((t,)), dma((t,)), dma((t,)), dma((t,)), dma((t,)),
            dma((t,)), dma((t,)),
            dma(()), dma(()), dma(()), dma(()), dma((3,)), dma((3,)), dma(()), dma(()),
            dma((4,)), dma((4,)), dma((4,)), dma((4,)),
        ],
        compiler_params=pltpu.CompilerParams(
            collective_id=0, has_side_effects=True, vmem_limit_bytes=48 * 1024 * 1024
        ),
    )(matrix.reshape(16, 8, 128, 128), small)
    return sketch, factors.reshape(16, 128, 128)


def solution(mesh):
    return jax.shard_map(
        body,
        mesh=mesh,
        in_specs=(P("rows", None), P("rows"), P("rows")),
        out_specs=(P("rows", None), P()),
        check_vma=False,
    )
```

```python
import functools
import math

import jax
import jax.numpy as jnp
from jax import lax
from jax.experimental import pallas as pl
from jax.experimental.pallas import tpu as pltpu
from jax.sharding import PartitionSpec as P

MESH = pl.DeviceIdType.MESH
F32 = jnp.float32
BF16 = jnp.bfloat16
I32 = jnp.int32

TICKS = 8
EARLY = 2
STREAMS = 4
ROWS = 2097152
SAMP_OWN = 2048


def dot_tt(lhs, rhs, precision=None):
    return lax.dot_general(
        lhs, rhs, (((0,), (0,)), ((), ())), precision=precision, preferred_element_type=F32
    )


def iota(shape, dim):
    return lax.broadcasted_iota(I32, shape, dim)


def odd(bits):
    bits = bits ^ (bits >> 4)
    bits = bits ^ (bits >> 2)
    bits = bits ^ (bits >> 1)
    return bits & 1


def split2(value):
    high = value.astype(BF16)
    return high, (value - high.astype(F32)).astype(BF16)


def split3(value):
    high = value.astype(BF16)
    rest = value - high.astype(F32)
    mid = rest.astype(BF16)
    return high, mid, (rest - mid.astype(F32)).astype(BF16)


def kernel(
    matrix_ref, small_ref, sketch_ref, factors_ref,
    X, SIB, P1, R1, R2, R3, R4, T3, R5, Y8, IDX, ML, OW, EB, FT, ET, POS, WF, WALL, G, RG1, RG2, GF, DUM,
    load_sem, y_send, y_recv, p_send, p_recv, sib_send, sib_recv,
    e_send, e_recv, x_send, x_recv, s1, r1, s2, r2, s3, r3, s4, r4, s5, r5,
    w_send, w_recv, g1_send, g1_recv, g2_send, g2_recv, g3_send, g3_recv,
    o_send, o_recv, f_send, f_recv,
):
    me = lax.axis_index("rows")
    core = me % 2
    y_pos = (me // 2) % 4
    x_pos = (me // 8) % 4
    z_pos = me // 32
    sibling = me + 1 - 2 * core

    def along(stride, hop):
        pos = (me // stride) % 4
        return me + ((pos + hop) % 4 - pos) * stride

    def send(src, dst, send_sem, recv_sem, device):
        copy = pltpu.make_async_remote_copy(
            src_ref=src, dst_ref=dst, send_sem=send_sem, recv_sem=recv_sem,
            device_id=(device,), device_id_type=MESH,
        )
        copy.start()

    def wait(ref, sem):
        pltpu.make_async_copy(ref, ref, sem).wait()

    def load(chunk):
        return pltpu.make_async_copy(matrix_ref.at[chunk], X.at[chunk], load_sem.at[chunk])

    for chunk in range(16):
        load(chunk).start()

    group = [(dy, dc) for dy in range(4) for dc in range(2) if (dy, dc) != (0, 0)]
    plane = [(dz, dx) for dz in range(4) for dx in range(4) if (dz, dx) != (0, 0)]

    def mate(dy, dc):
        return along(2, dy) + dc * (1 - 2 * core)

    def peer(dz, dx):
        return ((z_pos + dz) % 4) * 32 + ((x_pos + dx) % 4) * 8 + me % 8

    barrier = pltpu.get_barrier_semaphore()
    for dy, dc in group:
        pl.semaphore_signal(barrier, inc=1, device_id=(mate(dy, dc),), device_id_type=MESH)
    for dz, dx in plane:
        pl.semaphore_signal(barrier, inc=1, device_id=(peer(dz, dx),), device_id_type=MESH)

    had = (1 - 2 * odd(iota((128, 128), 0) & iota((128, 128), 1))).astype(F32)

    samples = small_ref[128:130, :]
    part = (samples >> 7) & 127
    intervals = jnp.concatenate([part[0:1], part[1:2]], axis=1)
    values = jnp.concatenate([samples[0:1], samples[1:2]], axis=1)
    onehot = iota((128, 256), 0) == intervals
    onehot_f = jnp.where(onehot, 1.0, 0.0)
    before = jnp.where(iota((256, 256), 0) < iota((256, 256), 1), 1.0, 0.0).astype(BF16)
    count = jnp.dot(onehot_f.astype(BF16), before, preferred_element_type=F32)
    rank = jnp.sum(count * onehot_f, axis=0, keepdims=True).astype(I32)
    place = (
        (intervals >> 6) * 128 + (intervals & 7) * 16 + ((intervals >> 3) & 7) * 2 + rank
    )
    POS[...] = place
    slot = rank * 128 + intervals
    chosen = jnp.where(iota((256, 256), 0) == slot, 1.0, 0.0).astype(BF16)
    row8 = iota((8, 256), 0)
    fields = jnp.where(row8 == 0, values & 127, jnp.where(row8 == 1, values >> 14, 0))
    sorted_fields = lax.dot_general(
        fields.astype(F32).astype(BF16), chosen, (((1,), (1,)), ((), ())), preferred_element_type=F32
    ).astype(I32)
    sorted_rows = (
        sorted_fields[1:2] * 16384 + (iota((1, 256), 1) & 127) * 128 + sorted_fields[0:1]
    )
    mine8 = 2 * y_pos + core
    Y8[mine8, 0:1, :] = sorted_rows[:, :128]
    Y8[mine8, 1:2, :] = sorted_rows[:, 128:]
    def front(chunk, carry):
        load(chunk).wait()
        for al in range(8):
            high, low = split2(X[chunk, al])
            sign = small_ref[pl.ds(chunk * 8 + al, 1), :].astype(F32)
            signed = (had * sign).astype(BF16)
            X[chunk, al] = jnp.dot(
                jnp.concatenate([signed, signed], axis=1),
                jnp.concatenate([high, low], axis=0),
                preferred_element_type=F32,
            )
        for tile in range(16):
            rows = slice(8 * tile, 8 * tile + 8)
            v = [X[chunk, al, rows, :] for al in range(8)]
            for span in (1, 2, 4):
                v = butterfly(v, span)
            for al in range(8):
                X[chunk, al, rows, :] = v[al]
        return carry

    def butterfly(v, span):
        out = list(v)
        for n in range(len(v)):
            if n & span == 0:
                out[n] = v[n] + v[n + span]
                out[n + span] = v[n] - v[n + span]
        return out

    lax.fori_loop(0, 4, front, 0, unroll=2)
    pl.semaphore_wait(barrier, 22)
    for n, (dy, dc) in enumerate(group):
        send(Y8.at[mine8], Y8.at[mine8], y_send.at[n], y_recv.at[n], mate(dy, dc))
    lax.fori_loop(4, 14, front, 0, unroll=2)
    for n in range(7):
        wait(Y8.at[0], y_recv.at[n])
    for q in range(8):
        for j in range(2):
            IDX[z_pos, x_pos, j, q : q + 1, :] = Y8[q, j : j + 1, :]
    for dz, dx in plane:
        send(IDX.at[z_pos, x_pos], IDX.at[z_pos, x_pos], p_send, p_recv, peer(dz, dx))
    lax.fori_loop(14, 16, front, 0, unroll=2)

    def second(step):
        def tile_step(tile, carry):
            rows = pl.ds(pl.multiple_of(tile * 8, 8), 8)
            v = [X[ah, step, rows, :] for ah in range(16)]
            for span in (1, 2, 4, 8):
                v = butterfly(v, span)
            for ah in range(16):
                X[ah, step, rows, :] = v[ah]
            return carry

        lax.fori_loop(0, 16, tile_step, 0, unroll=2)
        send(
            X.at[pl.ds((1 - core) * 8, 8), step], SIB.at[step], sib_send.at[step], sib_recv.at[step], sibling
        )

    def axis_of(order, stage):
        k = (order + stage) % 3
        stride = 32 - 33 * k + 9 * k * k
        return stride, (me // stride) % 4

    def block_of(s, q, sib):
        return SIB.at[q // 2, 2 * s + q % 2] if sib else X.at[core * 8 + 2 * s + q % 2, q // 2]

    def early_send(sib):
        for s in range(3):
            stride, a = axis_of(s, 0)
            for hop in (1, 2, 3):
                send(
                    block_of(s, (a + hop) % 4, sib), EB.at[s, a, sib], e_send.at[s], e_recv.at[s],
                    along(stride, hop),
                )

    second(0)
    second(1)
    early_send(0)
    second(2)
    second(3)
    wait(SIB.at[0], sib_recv.at[0])
    wait(SIB.at[1], sib_recv.at[1])
    early_send(1)
    for s in range(3):
        _, a = axis_of(s, 0)
        for sib in (0, 1):
            EB[s, a, sib] = block_of(s, a, sib)[...]
    for step in range(4, TICKS):
        second(step)

    wait(DUM, p_recv)
    from_t = iota((128, 128), 0)
    to_t = iota((128, 128), 1)
    hi_t, mid_t, lo_t, core_t = to_t // 32, (to_t // 8) % 4, (to_t // 2) % 4, to_t % 2
    natural = [
        hi_t * 32 + mid_t * 8 + lo_t * 2 + core_t,
        hi_t * 8 + mid_t * 2 + lo_t * 32 + core_t,
        hi_t * 2 + mid_t * 32 + lo_t * 8 + core_t,
    ]
    for order in range(3):
        perm = jnp.where(from_t == natural[order], 1.0, 0.0).astype(BF16)
        for j in range(2):
            rows = IDX[:, :, j].reshape(128, 128)
            low = (rows & 127).astype(F32).astype(BF16)
            block = (rows >> 14).astype(F32).astype(BF16)
            ML[order, j] = dot_tt(low, perm).astype(I32)
            OW[order, j] = dot_tt(block, perm).astype(I32)

    sub = iota((128, 128), 0)

    def order_of(s, tick):
        return s if s < 3 else tick % 3

    def picked(order, p, device, own, sib):
        picks = []
        for j in range(2):
            hit = sub == ML[order, j, pl.ds(p, 1), :]
            owner = OW[order, j, pl.ds(p, 1), :]
            for bits in (owner & device, owner & (device + 1 - 2 * core)):
                picks.append(jnp.where(hit, (1 - 2 * odd(bits)).astype(F32), 0.0).astype(BF16))
        pick = jnp.concatenate(
            [jnp.concatenate(picks[:2], axis=0), jnp.concatenate(picks[2:], axis=0)], axis=1
        )
        own_hi, own_lo = split2(own)
        sib_hi, sib_lo = split2(sib)
        terms = jnp.concatenate(
            [jnp.concatenate([own_hi, sib_hi], axis=0), jnp.concatenate([own_lo, sib_lo], axis=0)], axis=1
        )
        got = dot_tt(pick, terms)
        return got[:, :128] + got[:, 128:]

    def produce(tick, first):
        def one(n, carry):
            s = n // 2
            order = s + (s // 3) * (tick % 3 - 3)
            p = (core * 8 + n) * 8 + tick
            got = picked(order, p, me, X[core * 8 + n, tick], SIB[tick, n])
            P1[tick, s, n % 2] = got.reshape(2, 4, 4, 8, 128)
            return carry

        lax.fori_loop(first, 8, one, 0, unroll=8 - first)

    def produce_early(s, carry):
        stride, a = axis_of(s, 0)
        p = (core * 8 + 2 * s + a % 2) * 8 + a // 2
        wait(EB.at[0, pl.ds(0, 3)], e_recv.at[s])
        got = sum(picked(s, p, me + (q - a) * stride, EB[s, q, 0], EB[s, q, 1]) for q in range(4))
        got = got.reshape(2, 4, 4, 8, 128)
        for q in range(4):
            for j in range(2):
                P1[q // 2, s, q % 2, j, a] = got[j, q]
        return carry

    def spread(tick, s, slabs, far, sems, stride, pos):
        over = (pos + 2) % 4
        for half, hop in ((0, 1), (1, 3)):
            send(slabs(over).at[:, half], far.at[tick, s, :, half], *sems, along(stride, hop))

    def relay(tick, s, slabs, near, far, sems, stride, pos):
        near_send, near_recv = sems
        for slot, hop in ((0, 1), (1, 3)):
            slab = slabs((pos + hop) % 4)
            slab[:, slot] += far[tick, s, :, slot]
            send(slab, near.at[tick, s, slot], near_send, near_recv, along(stride, hop))

    def slabs_of(tick, s):
        return lambda q: P1.at[tick, s, :, :, q]

    def parts_of(tick, s, a):
        return lambda q: P1.at[tick, s, :, :, a, q]

    def wait_streams(ref, sem, tick, streams):
        wait(ref.at[tick] if len(streams) == STREAMS else ref.at[tick, 3], sem.at[tick])

    def first_send(tick, streams):
        for s in streams:
            spread(tick, s, slabs_of(tick, s), R1, (s1.at[tick], r1.at[tick]), *axis_of(order_of(s, tick), 0))

    def first_pass(tick, streams):
        wait_streams(R1, r1, tick, streams)
        for s in streams:
            sems = (s2.at[tick], r2.at[tick])
            relay(tick, s, slabs_of(tick, s), R2, R1, sems, *axis_of(order_of(s, tick), 0))

    def second_send(tick, streams):
        wait_streams(R2, r2, tick, streams)
        for s in range(STREAMS):
            _, a = axis_of(order_of(s, tick), 0)
            if s in streams:
                P1[tick, s, :, :, a] += R2[tick, s, 0] + R2[tick, s, 1]
            spread(tick, s, parts_of(tick, s, a), R3, (s3.at[tick], r3.at[tick]), *axis_of(order_of(s, tick), 1))

    def second_pass(tick, streams):
        wait(R3.at[tick], r3.at[tick])
        for s in range(STREAMS):
            _, a = axis_of(order_of(s, tick), 0)
            sems = (s4.at[tick], r4.at[tick])
            relay(tick, s, parts_of(tick, s, a), R4, R3, sems, *axis_of(order_of(s, tick), 1))

    def third_send(tick, streams):
        wait(R4.at[tick], r4.at[tick])
        for s in range(STREAMS):
            _, a = axis_of(order_of(s, tick), 0)
            _, b = axis_of(order_of(s, tick), 1)
            total = P1[tick, s, :, :, a, b] + R4[tick, s, 0] + R4[tick, s, 1]
            for g in range(2):
                for j in range(2):
                    for q in range(4):
                        for ct in range(2):
                            row = ct * 4 + g * 2 + j
                            T3[tick, s, q, row : row + 1, :] = total[g, j, 2 * q + ct : 2 * q + ct + 1, :]
            stride, d = axis_of(order_of(s, tick), 2)
            for hop in (1, 2, 3):
                send(
                    T3.at[tick, s, (d + hop) % 4], R5.at[tick, s, hop - 1], s5.at[tick], r5.at[tick],
                    along(stride, hop),
                )

    scale = 1.0 / math.sqrt(ROWS)

    def last(tick, streams):
        wait(R5.at[tick], r5.at[tick])
        done = []
        for s in range(STREAMS):
            _, d = axis_of(order_of(s, tick), 2)
            done.append((T3[tick, s, d] + R5[tick, s, 0] + R5[tick, s, 1] + R5[tick, s, 2]) * scale)
            if s not in streams:
                FT[tick, s] = done[s]
        if len(streams) < STREAMS:
            for ct in range(2):
                WF[ct, pl.ds(pl.multiple_of(tick * 16 + 8, 8), 8), :] = jnp.concatenate(
                    [done[3][4 * ct : 4 * ct + 4]] * 2, axis=0
                )
            return
        for ct in range(2):
            for pair in range(2):
                rows = pl.ds(pl.multiple_of(tick * 16 + pair * 8, 8), 8)
                WF[ct, rows, :] = jnp.concatenate(
                    [done[2 * pair][4 * ct : 4 * ct + 4], done[2 * pair + 1][4 * ct : 4 * ct + 4]], axis=0
                )

    def make(tick, streams):
        if len(streams) == STREAMS:
            wait(SIB.at[tick], sib_recv.at[tick])
        produce(tick, 2 * streams[0])
        first_send(tick, streams)

    everything, late = (0, 1, 2, 3), (3,)

    def each(work, start, stop, streams):
        def step(tick, carry):
            work(tick, streams)
            return carry

        lax.fori_loop(start, stop, step, 0)

    for work in (make, first_pass, second_send, second_pass, third_send, last):
        each(work, 0, EARLY, late)
        if work is last:
            for s in range(3):
                stride, a = axis_of(s, 0)
                for hop in (1, 2, 3):
                    send(FT.at[((a + hop) % 4) // 2, s], ET.at[s, a], x_send.at[s], x_recv.at[s], along(stride, hop))
                ET[s, a] = FT[a // 2, s]
        each(work, EARLY, TICKS, everything)
        if work is first_pass:
            lax.fori_loop(0, 3, produce_early, 0)

    for s in range(3):
        wait(ET.at[0, pl.ds(0, 3)], x_recv.at[s])
    for tick in range(EARLY):
        for ct in range(2):
            rows = []
            for s in range(3):
                _, a = axis_of(s, 0)
                for g in range(2):
                    tile = ET[s, 2 * tick + g]
                    pair = [tile[4 * ct + 2 * n : 4 * ct + 2 * n + 2] for n in range(2)]
                    rows.append(jnp.where(a % 2 == 0, pair[0], pair[1]))
            rows.append(WF[ct, 16 * tick + 12 : 16 * tick + 16, :])
            WF[ct, 16 * tick : 16 * tick + 16, :] = jnp.concatenate(rows, axis=0)

    send(WF.at[1 - core], WALL.at[core], w_send, w_recv, sibling)
    high, low = split2(WF[...].reshape(256, 128))
    square = dot_tt(high, jnp.concatenate([high, low], axis=1))
    gram = square[:, :128] + (square[:, 128:] + square[:, 128:].T)
    G[...] = (gram * (1.0 / SAMP_OWN)).reshape(2, 64, 128)
    send(G.at[1 - core], RG1, g1_send, g1_recv, sibling)
    wait(RG1, g1_recv)
    G[core] += RG1[...]
    for hop in (1, 2, 3):
        send(G.at[core], RG2.at[hop - 1], g2_send.at[hop - 1], g2_recv.at[hop - 1], along(2, hop))

    WALL[core] = WF[core]
    wait(WALL.at[0], w_recv)
    back = jnp.where(iota((256, 256), 0) == POS[...], 1.0, 0.0).astype(BF16)
    sketch_ref[...] = sum(dot_tt(back, term) for term in split3(WALL[...].reshape(256, 128)))

    for hop in (1, 2, 3):
        wait(RG2.at[0], g2_recv.at[hop - 1])
    terms = [G[core], RG2[0], RG2[1], RG2[2]]
    GF[core] = (terms[0] + terms[2]) + (terms[1] + terms[3])
    send(GF.at[core], GF.at[core], g3_send, g3_recv, sibling)
    wait(GF.at[0], g3_recv)

    sub16 = iota((16, 128), 0)
    lane16 = iota((16, 128), 1)
    work = GF[...].reshape(128, 128)
    for r in range(8):
        panel = work[:16]
        columns = [jnp.broadcast_to(panel[:, 16 * r + k : 16 * r + k + 1], (16, 128)) for k in range(16)]
        scales = jnp.zeros((16, 128), F32)
        for j in range(16):
            inverse = lax.rsqrt(columns[j][j : j + 1])
            square = inverse * inverse
            below = jnp.where(sub16 > j, columns[j], 0.0)
            scales = jnp.where(sub16 == j, inverse, scales)
            for k in range(j + 1, 16):
                columns[k] = columns[k] - (below * columns[k][j : j + 1]) * square
            panel = panel - (below * panel[j : j + 1]) * square
        panel = jnp.where(lane16 >= 16 * r + sub16, panel * scales, 0.0)

        @pl.when(core == r % 2)
        def _():
            factors_ref[z_pos, x_pos, r] = panel
            block = factors_ref.at[z_pos, x_pos, r]
            for dz, dx in plane:
                send(block, block, o_send.at[r // 2], o_recv.at[r // 2], peer(dz, dx))

        if r < 7:
            h, m, l = (term.astype(F32) for term in split3(panel))
            lhs = jnp.concatenate([h, h, m, m, h, l], axis=0).astype(BF16)
            rhs = jnp.concatenate([h, m, h, m, l, h], axis=0).astype(BF16)
            work = work[16:] - dot_tt(lhs, rhs)[16 * r + 16 :]

    def share(n):
        slab = factors_ref.at[:, :, 2 * n + core]
        wait(DUM, o_recv.at[n])
        send(slab, slab, f_send.at[n], f_recv.at[n], sibling)

    for n in range(2):
        share(n)

    for n in range(7):
        wait(Y8.at[0], y_send.at[n])
    wait(DUM, p_send)
    for n in range(3):
        wait(RG2.at[0], g2_send.at[n])
    wait(GF.at[0], g3_send)
    wait(RG1, g1_send)
    wait(WALL.at[0], w_send)

    for s in range(3):
        wait(EB.at[0, pl.ds(0, 3)], e_send.at[s])
        wait(ET.at[0, pl.ds(0, 3)], x_send.at[s])

    def sent(tick, streams):
        wait(SIB.at[tick], sib_send.at[tick])
        wait_streams(R1, s1, tick, streams)
        wait_streams(R2, s2, tick, streams)
        wait(R3.at[tick], s3.at[tick])
        wait(R4.at[tick], s4.at[tick])
        wait(R5.at[tick], s5.at[tick])

    each(sent, 0, EARLY, late)
    each(sent, EARLY, TICKS, everything)

    for n in range(2, 4):
        share(n)
    for n in range(4):
        wait(factors_ref.at[:, :, 0], f_recv.at[n])
    for n in range(4):
        wait(DUM, o_send.at[n])
        wait(factors_ref.at[:, :, 0], f_send.at[n])


def body(matrix, signs, samples):
    dma = pltpu.SemaphoreType.DMA
    vmem = pltpu.VMEM
    t, s = TICKS, STREAMS
    small = jnp.concatenate([signs, samples]).reshape(130, 128)
    sketch, factors = pl.pallas_call(
        kernel,
        out_shape=(
            jax.ShapeDtypeStruct((256, 128), F32),
            jax.ShapeDtypeStruct((4, 4, 8, 16, 128), F32),
        ),
        in_specs=[pl.BlockSpec(memory_space=pltpu.HBM), pl.BlockSpec(memory_space=pltpu.VMEM)],
        out_specs=(pl.BlockSpec(memory_space=pltpu.VMEM), pl.BlockSpec(memory_space=pltpu.VMEM)),
        scratch_shapes=[
            vmem((16, 8, 128, 128), F32),
            vmem((8, 8, 128, 128), F32),
            vmem((t, s, 2, 2, 4, 4, 8, 128), F32),
            vmem((t, s, 2, 2, 4, 8, 128), F32),
            vmem((t, s, 2, 2, 2, 4, 8, 128), F32),
            vmem((t, s, 2, 2, 8, 128), F32),
            vmem((t, s, 2, 2, 2, 8, 128), F32),
            vmem((t, s, 4, 8, 128), F32),
            vmem((t, s, 3, 8, 128), F32),
            vmem((8, 8, 128), I32),
            vmem((4, 4, 2, 8, 128), I32),
            vmem((3, 2, 128, 128), I32),
            vmem((3, 2, 128, 128), I32),
            vmem((3, 4, 2, 128, 128), F32),
            vmem((2, 3, 8, 128), F32),
            vmem((3, 4, 8, 128), F32),
            vmem((1, 256), I32),
            vmem((2, 128, 128), F32),
            vmem((2, 128, 128), F32),
            vmem((2, 64, 128), F32),
            vmem((64, 128), F32),
            vmem((3, 64, 128), F32),
            vmem((2, 64, 128), F32),
            vmem((15, 16, 128), F32),
            dma((16,)), dma((7,)), dma((7,)), dma(()), dma(()),
            dma((t,)), dma((t,)),
            dma((3,)), dma((3,)), dma((3,)), dma((3,)),
            dma((t,)), dma((t,)), dma((t,)), dma((t,)), dma((t,)), dma((t,)), dma((t,)), dma((t,)),
            dma((t,)), dma((t,)),
            dma(()), dma(()), dma(()), dma(()), dma((3,)), dma((3,)), dma(()), dma(()),
            dma((4,)), dma((4,)), dma((4,)), dma((4,)),
        ],
        compiler_params=pltpu.CompilerParams(
            collective_id=0, has_side_effects=True, vmem_limit_bytes=48 * 1024 * 1024
        ),
    )(matrix.reshape(16, 8, 128, 128), small)
    return sketch, factors.reshape(16, 128, 128)


def solution(mesh):
    return jax.shard_map(
        body,
        mesh=mesh,
        in_specs=(P("rows", None), P("rows"), P("rows")),
        out_specs=(P("rows", None), P()),
        check_vma=False,
    )
```
